256 devices in a mesh: frames: 8 (over x, y_hi), rows: 32 (over z, y_lo, core).
Axes of the slice: x: 4, y: 4 (y_hi: 2, y_lo: 2; y = y_hi * 2 + y_lo), z: 8, core: 2. Of those that a mesh axis runs over, the one named last changes fastest.
Arguments:
- series: bfloat16 [128, 1, 256, 256], P('frames', None, 'rows'), may hold values from -6 to 6
- lift_weight: bfloat16 [3, 3, 2, 64], replicated, may hold values from -1.5 to 1.5
- lift_bias: float32 [64], replicated, may hold values from -3 to 3
- mix_weight: bfloat16 [3, 3, 64, 64], replicated, may hold values from -0.25 to 0.25
- mix_bias: float32 [64], replicated, may hold values from -3 to 3
- proj_weight: bfloat16 [64, 2], replicated, may hold values from -0.75 to 0.75
- proj_bias: float32 [2], replicated, may hold values from -3 to 3
Outputs:
- refined: float32 [128, 1, 256, 256], P('frames', None, 'rows')
The draws below stay inside these ranges and needn't reach their ends.
All inputs are finite; a program needn't handle non-finite values.
Results may differ from the reference program's by a relative error of at most 0.007.
Values may be sent and summed in bfloat16 or wider, within the bound.
A program may use at most 192 MiB of HBM per device.

```python
import math
import jax
import jax.numpy as jnp
from jax import lax

HID = 64
FRAME_DEV = 16
COLS = 128
SLICES = 1
NFRAME = 128
NROW = 256
N_FRAMES = 8


def shard_levels(stream_key, dims, pieces, smallest, top_value):
    def one(dim, shards_of):
        heights = jax.random.uniform(jax.random.fold_in(jax.random.fold_in(stream_key, 6), dim), (shards_of,), jnp.float32, smallest / len(pieces), top_value / len(pieces))
        return jnp.repeat(jnp.exp(heights), dims[dim] // shards_of).reshape((-1,) + (1,) * (len(dims) - dim - 1))

    gain = one(*pieces[0])
    for cut in pieces[1:]:
        gain = gain * one(*cut)
    return gain


def centred(rng, dims, width, bound, split=(), held_as=jnp.bfloat16):
    drawn = jax.random.normal(rng, dims, jnp.float32) * width
    if len(split) > 0:
        drawn = shard_levels(rng, dims, split, -0.22, 0.18) * drawn
    return jnp.clip(drawn, min=-bound, max=bound).astype(held_as)


def setup_inputs(seed: int = 0) -> dict:
    key_of = jax.random.split(jax.random.key(seed), 8)
    series = centred(key_of[0], (NFRAME, SLICES, NROW, 2 * COLS), 1.0, 6.0, ((0, 8), (2, 32)))
    lift_weight = centred(key_of[1], (3, 3, 2, HID), 18 ** -0.5, 1.5)
    lift_bias = centred(key_of[2], (HID,), 0.5, 3.0, (), jnp.float32)
    mix_weight = centred(key_of[3], (3, 3, HID, HID), (9 * HID) ** -0.5, 0.25)
    mix_bias = centred(key_of[4], (HID,), 0.5, 3.0, (), jnp.float32)
    proj_weight = centred(key_of[5], (HID, 2), HID ** -0.5, 0.75)
    proj_bias = centred(key_of[6], (2,), 0.5, 3.0, (), jnp.float32)
    return {"series": series, "lift_weight": lift_weight, "lift_bias": lift_bias, "mix_weight": mix_weight, "mix_bias": mix_bias, "proj_weight": proj_weight, "proj_bias": proj_bias}


def phases(freq_idx, time_idx, total):
    wrapped = jnp.remainder((freq_idx[:, None] - total // 2) * time_idx[None, :], total)
    return 2.0 * math.pi / total * wrapped.astype(jnp.float32)

def fwd_table(freq_idx, time_idx, total):
    angles = phases(freq_idx, time_idx, total)
    factor = 1.0 / math.sqrt(total)
    return jnp.concatenate([jnp.cos(angles) * factor, -jnp.sin(angles) * factor], 0).astype(jnp.bfloat16)

def inv_table(time_idx, freq_idx, total):
    angles = phases(freq_idx, time_idx, total).T
    factor = 1.0 / math.sqrt(total)
    return jnp.concatenate([jnp.cos(angles) * factor, jnp.sin(angles) * factor], 0).astype(jnp.bfloat16)

def apply_table(table, values):
    height = table.shape[0] // 2
    flattened = values.reshape(values.shape[0], -1)
    product = jnp.dot(table, flattened, preferred_element_type=jnp.float32)
    product = product.reshape((2, height) + values.shape[1:])
    half_cols = values.shape[-1] // 2
    lower_part = product[1]
    return product[0] + jnp.concatenate([-lower_part[..., half_cols:], lower_part[..., :half_cols]], -1)

def conv_first(region, lift_weight, lift_bias, keep_mask):
    n_freq = region.shape[0] - 2
    n_rows = region.shape[1] - 2
    half_cols = region.shape[2] // 2
    split_in = region.reshape(n_freq + 2, n_rows + 2, 2, half_cols).astype(jnp.float32)
    running = jnp.zeros((n_freq, n_rows, lift_weight.shape[3], half_cols), jnp.float32)
    for tap_row in range(3):
        for tap_col in range(3):
            running = running + jnp.einsum('io,kric->kroc', lift_weight[tap_row, tap_col].astype(jnp.float32), split_in[tap_row:tap_row + n_freq, tap_col:tap_col + n_rows])
    hidden = jax.nn.relu(running + lift_bias[None, None, :, None])
    hidden = hidden * keep_mask[:, :, None, None]
    return hidden.astype(jnp.bfloat16)

def conv_rest(padded, mix_weight, mix_bias, proj_weight, proj_bias):
    n_freq = padded.shape[0] - 2
    n_rows = padded.shape[1] - 2
    running = jnp.zeros((n_freq, n_rows, mix_weight.shape[3], padded.shape[3]), jnp.float32)
    for tap_row in range(3):
        for tap_col in range(3):
            running = running + jnp.einsum('io,kric->kroc', mix_weight[tap_row, tap_col].astype(jnp.float32), padded[tap_row:tap_row + n_freq, tap_col:tap_col + n_rows].astype(jnp.float32))
    mixed = jax.nn.relu(running + mix_bias[None, None, :, None]).astype(jnp.bfloat16)
    update = jnp.einsum('io,kric->kroc', proj_weight.astype(jnp.float32), mixed.astype(jnp.float32)) + proj_bias[None, None, :, None]
    return update.reshape(n_freq, n_rows, 2 * padded.shape[3]).astype(jnp.bfloat16)

def reference(series, lift_weight, lift_bias, mix_weight, mix_bias, proj_weight, proj_bias):
    freq_idx = jnp.arange(NFRAME, dtype=jnp.int32)
    spectrum = apply_table(fwd_table(freq_idx, freq_idx, NFRAME), series).astype(jnp.bfloat16)
    updates = []
    for slice_idx in range(SLICES):
        padded_in = jnp.pad(spectrum[:, slice_idx], ((2, 2), (2, 2), (0, 0)))

        def one_block(block_idx):
            start_freq = (block_idx * FRAME_DEV).astype(jnp.int32)
            region = lax.dynamic_slice(padded_in, (start_freq, jnp.int32(0), jnp.int32(0)), (FRAME_DEV + 4, NROW + 4, 2 * COLS))
            freq_pos = start_freq - 1 + jnp.arange(FRAME_DEV + 2, dtype=jnp.int32)
            row_pos = jnp.arange(NROW + 2, dtype=jnp.int32) - 1
            inside = ((freq_pos >= 0) & (freq_pos < NFRAME))[:, None] & ((row_pos >= 0) & (row_pos < NROW))[None, :]
            hidden = conv_first(region, lift_weight, lift_bias, inside.astype(jnp.float32))
            return conv_rest(hidden, mix_weight, mix_bias, proj_weight, proj_bias)
        blocks = lax.map(one_block, jnp.arange(N_FRAMES, dtype=jnp.int32))
        updates.append(blocks.reshape(NFRAME, NROW, 2 * COLS))
    update = jnp.stack(updates, 1)
    return series.astype(jnp.float32) + apply_table(inv_table(freq_idx, freq_idx, NFRAME), update)
```

```python
import functools
import math

import jax
import jax.numpy as jnp
import ml_dtypes
import numpy as np
from jax import lax
from jax.experimental import pallas as pl
from jax.experimental.pallas import tpu as pltpu
from jax.sharding import PartitionSpec as P

MESH = pl.DeviceIdType.MESH
BF16 = jnp.bfloat16
F32 = jnp.float32

NF = 8
T = 16
N = 128
R = 8
C = 16
O = 64
KB = 4
NB = N // KB
G = 16
NG = N // G
W = G + 2


def forward_table():
    k = np.arange(N)
    t = np.arange(N)
    angle = (2.0 * math.pi / N * (((k[:, None] - N // 2) * t[None, :]) % N)).astype(np.float32)
    scale = np.float32(1.0 / math.sqrt(N))
    re = (np.cos(angle) * scale).astype(ml_dtypes.bfloat16).astype(np.float32)
    im = (-np.sin(angle) * scale).astype(ml_dtypes.bfloat16).astype(np.float32)
    full = np.zeros((NF, 2, T, NG, 128), np.float32)
    for g in range(NG):
        for w in range(W):
            kk = g * G + w - 1
            if not 0 <= kk < N:
                continue
            a = re[kk].reshape(NF, T)
            b = im[kk].reshape(NF, T)
            for tap in range(3):
                lane = tap * 2 * W + w * 2
                full[:, 0, :, g, lane] = a
                full[:, 1, :, g, lane] = -b
                full[:, 0, :, g, lane + 1] = b
                full[:, 1, :, g, lane + 1] = a
    return full.reshape(NF * 2 * T, NG * 128).astype(ml_dtypes.bfloat16)


def inverse_table():
    k = np.arange(N)
    t = np.arange(N)
    angle = (2.0 * math.pi / N * (((k[:, None] - N // 2) * t[None, :]) % N)).astype(np.float32).T
    scale = np.float32(1.0 / math.sqrt(N))
    re = (np.cos(angle) * scale).reshape(NF, T, N)
    im = (np.sin(angle) * scale).reshape(NF, T, N)
    full = np.zeros((NF, 2, T, N, 2), np.float32)
    full[:, 0, :, :, 0] = re
    full[:, 0, :, :, 1] = -im
    full[:, 1, :, :, 0] = im
    full[:, 1, :, :, 1] = re
    return full.reshape(NF * 2 * T, N * 2).astype(ml_dtypes.bfloat16)


def place_table():
    full = np.zeros((G // KB, 128, KB, 32), np.float32)
    for q in range(G // KB):
        for j in range(KB):
            for a in range(3):
                for b in range(3):
                    for i in range(2):
                        full[q, b * 2 * W + (q * KB + j + a) * 2 + i, j, (a * 3 + b) * 2 + i] = 1
    return full.reshape(G // KB, 128, 128).astype(ml_dtypes.bfloat16)


def butterfly(parts):
    lane = lax.broadcasted_iota(jnp.int32, parts[0].shape, 1)
    for bit in range(3):
        step = 1 << bit
        upper = ((lane >> (4 + bit)) & 1) == 1
        out = list(parts)
        for i in range(8):
            if i & step:
                continue
            lo, hi = parts[i], parts[i + step]
            out[i] = jnp.where(upper, pltpu.roll(hi, 16 * step, 1), lo)
            out[i + step] = jnp.where(upper, hi, pltpu.roll(lo, 128 - 16 * step, 1))
        parts = out
    return parts


def kernel(
    n_rows,
    series,
    fwd,
    inv,
    place,
    lift4,
    lift_bias,
    mix,
    mix_bias,
    proj,
    proj_bias,
    out,
    series_v,
    fwd_v,
    inv_v,
    place_v,
    lift4_v,
    lift_bias_v,
    mix_v,
    mix_bias_v,
    proj_v,
    proj_bias_v,
    series_f,
    sent,
    got,
    xt,
    halo,
    spec,
    patch_a,
    patch_b,
    lift_m,
    mix_m,
    hid,
    upd,
    sent2,
    got2,
    load_sem,
    send_sem,
    recv_sem,
    halo_send_sem,
    halo_recv_sem,
    send2_sem,
    recv2_sem,
):
    f = lax.axis_index("frames")
    r = lax.axis_index("rows")
    above = lax.rem(r + n_rows - 1, n_rows)
    below = lax.rem(r + 1, n_rows)
    peers = [lax.rem(f + d, NF) for d in range(1, NF)]

    barrier = pltpu.get_barrier_semaphore()
    for p in peers:
        pl.semaphore_signal(barrier, inc=1, device_id={"frames": p}, device_id_type=MESH)
    for p in (above, below):
        pl.semaphore_signal(barrier, inc=1, device_id={"rows": p}, device_id_type=MESH)

    loads = [
        pltpu.make_async_copy(a, b, load_sem.at[i])
        for i, (a, b) in enumerate(
            (
                (series, series_v),
                (mix, mix_v),
                (lift4, lift4_v),
                (place, place_v),
                (fwd, fwd_v),
                (inv, inv_v),
                (lift_bias, lift_bias_v),
                (mix_bias, mix_bias_v),
                (proj, proj_v),
                (proj_bias, proj_bias_v),
            )
        )
    ]
    for c in loads:
        c.start()

    loads[0].wait()
    for ri in range(2):
        series_f[ri] = series_v[:, 0, :, ri * 128 : ri * 128 + 128].astype(F32).reshape(T * R, 128)
    for ri in range(2):
        parts = [series_f[ri, pl.ds(i, T, stride=R), :] for i in range(R)]
        for i, part in enumerate(butterfly(parts)):
            sent[i, ri * T : ri * T + T, :] = part.astype(BF16)

    pl.semaphore_wait(barrier, NF + 1)
    first = [
        pltpu.make_async_remote_copy(
            src_ref=sent.at[p],
            dst_ref=got.at[f],
            send_sem=send_sem.at[i],
            recv_sem=recv_sem.at[i],
            device_id={"frames": p},
            device_id_type=MESH,
        )
        for i, p in enumerate(peers)
    ]
    for c in first:
        c.start()
    got[f] = sent[f]

    for c in loads[1:]:
        c.wait()
    for q in range(G // KB):
        lift_m[:, q * 256 : q * 256 + 256] = jnp.dot(
            place_v[q], lift4_v[...], preferred_element_type=F32
        ).astype(BF16)
    zero = jnp.zeros((O, O), BF16)
    for b in range(3):
        t0, t1, t2 = (mix_v[a, b] for a in range(3))
        rows = (
            (t1, t0, zero, zero),
            (t2, t1, t0, zero),
            (zero, t2, t1, t0),
            (zero, zero, t2, t1),
        )
        for j, row in enumerate(rows):
            mix_m[b * 256 + j * O : b * 256 + j * O + O, :] = jnp.concatenate(row, axis=1)
        mix_m[768 + b * 128 : 768 + b * 128 + O, :] = jnp.concatenate((zero, zero, zero, t2), axis=1)
        mix_m[768 + b * 128 + O : 768 + b * 128 + 128, :] = jnp.concatenate((t0, zero, zero, zero), axis=1)
    hid[0] = jnp.zeros(hid.shape[1:], BF16)
    hid[NB + 1] = jnp.zeros(hid.shape[1:], BF16)

    for c in first:
        c.wait_recv()
    xt[...] = got[...].reshape(256, 128).T

    halos = [
        pltpu.make_async_remote_copy(
            src_ref=xt.at[pl.ds(lo, 2 * C)],
            dst_ref=halo.at[i],
            send_sem=halo_send_sem.at[i],
            recv_sem=halo_recv_sem.at[i],
            device_id={"rows": p},
            device_id_type=MESH,
        )
        for i, (lo, p) in enumerate(((6 * C, below), (0, above)))
    ]
    for c in halos:
        c.start()

    own = jnp.dot(xt[...], fwd_v[...], preferred_element_type=F32).astype(BF16)
    for g in range(NG):
        spec[g, 2 * C : 10 * C, :] = own[:, g * 128 : g * 128 + 128]

    def gather(g, lo, size):
        lane = lax.broadcasted_iota(jnp.int32, (size, 128), 1)
        rows = [spec[g, lo + b * C : lo + b * C + size, :] for b in range(3)]
        return jnp.where(lane < 2 * W, rows[0], jnp.where(lane < 4 * W, rows[1], rows[2]))

    def lift(patch):
        return [
            jnp.maximum(
                jnp.dot(patch, lift_m[:, q * 256 : q * 256 + 256], preferred_element_type=F32)
                + lift_bias_v[:, q * 256 : q * 256 + 256],
                0.0,
            )
            for q in range(G // KB)
        ]

    for g in range(NG):
        for q, h in enumerate(lift(gather(g, 2 * C, 6 * C))):
            hid[g * KB + q + 1, 2 * C : 8 * C, :] = h.astype(BF16)

    for c in halos:
        c.wait_recv()
    top = jnp.where(r > 0, halo[0], jnp.zeros_like(halo[0]))
    bottom = jnp.where(r < n_rows - 1, halo[1], jnp.zeros_like(halo[1]))
    outer = jnp.dot(
        jnp.concatenate((top, bottom), axis=0), fwd_v[...], preferred_element_type=F32
    ).astype(BF16)
    for g in range(NG):
        spec[g, : 2 * C, :] = outer[: 2 * C, g * 128 : g * 128 + 128]
        spec[g, 10 * C :, :] = outer[2 * C :, g * 128 : g * 128 + 128]

    row = lax.broadcasted_iota(jnp.int32, (4 * C, 256), 0)
    keep = ((row >= C) | (r > 0)) & ((row < 3 * C) | (r < n_rows - 1))
    for g in range(NG):
        patch = jnp.concatenate((gather(g, 0, 2 * C), gather(g, 8 * C, 2 * C)), axis=0)
        for q, h in enumerate(lift(patch)):
            h = jnp.where(keep, h, 0.0).astype(BF16)
            hid[g * KB + q + 1, : 2 * C, :] = h[: 2 * C]
            hid[g * KB + q + 1, 8 * C :, :] = h[2 * C :]

    lane = lax.broadcasted_iota(jnp.int32, (10 * C, 128), 1)

    def block(g, carry):
        total = None
        edges = []
        for q in range(KB):
            kb = g * KB + q + 1
            edges.append(
                jnp.where(lane < O, hid[kb + 1, :, :128], hid[kb - 1, :, 128:])
            )
        for b in range(3):
            rows = jnp.concatenate(
                [hid[g * KB + q + 1, b * C : b * C + 8 * C, :] for q in range(KB)], axis=0
            )
            part = jnp.dot(rows, mix_m[b * 256 : b * 256 + 256, :], preferred_element_type=F32)
            total = part if total is None else total + part
        rows = jnp.concatenate(
            [
                jnp.concatenate([e[b * C : b * C + 8 * C] for b in range(3)], axis=1)
                for e in edges
            ],
            axis=0,
        )
        total = total + jnp.dot(rows, mix_m[768:, :], preferred_element_type=F32)
        mixed = jnp.maximum(total + mix_bias_v[...], 0.0).astype(BF16)
        u = lax.dot_general(
            proj_v[...], mixed, (((1,), (1,)), ((), ())), preferred_element_type=F32
        )
        for q in range(KB):
            lo = pl.multiple_of((g * KB + q) * 8, 8)
            upd[pl.ds(lo, 8), :] = u[:, q * 128 : q * 128 + 128] + proj_bias_v[...]
        return carry

    lax.fori_loop(0, NB // KB, block, 0)

    back = jnp.dot(inv_v[...], upd[...].astype(BF16), preferred_element_type=F32)
    sent2[...] = back.astype(BF16).reshape(NF, 2 * T, 128)

    second = [
        pltpu.make_async_remote_copy(
            src_ref=sent2.at[p],
            dst_ref=got2.at[f],
            send_sem=send2_sem.at[i],
            recv_sem=recv2_sem.at[i],
            device_id={"frames": p},
            device_id_type=MESH,
        )
        for i, p in enumerate(peers)
    ]
    for c in second:
        c.start()
    got2[f] = sent2[f]
    for c in first + halos:
        c.wait_send()
    for c in second:
        c.wait_recv()
    for ri in range(2):
        parts = [got2[i, ri * T : ri * T + T, :].astype(F32) for i in range(NF)]
        for i, part in enumerate(butterfly(parts)):
            at = (ri, pl.ds(i, T, stride=R), slice(None))
            out[at] = part + series_f[at]
    for c in second:
        c.wait_send()


def per_device(series, lift_weight, lift_bias, mix_weight, mix_bias, proj_weight, proj_bias):
    n_rows = lax.axis_size("rows")
    lift4 = jnp.pad(lift_weight.reshape(18, O), ((0, 14), (0, 0)))
    eye = jnp.eye(KB, dtype=BF16)
    lift4 = (eye[:, None, :, None] * lift4[None, :, None, :]).reshape(KB * 32, KB * O)
    proj = (eye[:, None, :, None] * proj_weight.T[None, :, None, :]).reshape(KB * 2, KB * O)
    args = (
        series,
        jnp.asarray(forward_table()),
        jnp.asarray(inverse_table()),
        jnp.asarray(place_table()),
        lift4,
        jnp.tile(lift_bias, G)[None],
        mix_weight,
        jnp.tile(mix_bias, KB)[None],
        proj,
        jnp.broadcast_to(jnp.tile(proj_bias, KB)[:, None], (8, 128)),
    )
    scratch = [pltpu.VMEM(a.shape, a.dtype) for a in args]
    scratch[0] = pltpu.VMEM((T, 1, R, 256), BF16)
    out = pl.pallas_call(
        functools.partial(kernel, n_rows),
        out_shape=jax.ShapeDtypeStruct((2, T * R, 128), F32),
        in_specs=[pl.BlockSpec(memory_space=pl.ANY)] * len(args),
        out_specs=pl.BlockSpec(memory_space=pltpu.VMEM),
        scratch_shapes=scratch
        + [
            pltpu.VMEM((2, T * R, 128), F32),
            pltpu.VMEM((NF, 2 * T, 128), BF16),
            pltpu.VMEM((NF, 2 * T, 128), BF16),
            pltpu.VMEM((R * C, 256), BF16),
            pltpu.VMEM((2, 2 * C, 256), BF16),
            pltpu.VMEM((NG, 12 * C, 128), BF16),
            pltpu.VMEM((NG, 6 * C, 128), BF16),
            pltpu.VMEM((NG, 4 * C, 128), BF16),
            pltpu.VMEM((128, G * O), BF16),
            pltpu.VMEM((1152, 256), BF16),
            pltpu.VMEM((NB + 2, 10 * C, 256), BF16),
            pltpu.VMEM((2 * N, 128), F32),
            pltpu.VMEM((NF, 2 * T, 128), BF16),
            pltpu.VMEM((NF, 2 * T, 128), BF16),
            pltpu.SemaphoreType.DMA((len(args),)),
            pltpu.SemaphoreType.DMA((NF - 1,)),
            pltpu.SemaphoreType.DMA((NF - 1,)),
            pltpu.SemaphoreType.DMA((2,)),
            pltpu.SemaphoreType.DMA((2,)),
            pltpu.SemaphoreType.DMA((NF - 1,)),
            pltpu.SemaphoreType.DMA((NF - 1,)),
        ],
        compiler_params=pltpu.CompilerParams(
            collective_id=0, has_side_effects=True, vmem_limit_bytes=40 * 1024 * 1024
        ),
    )(*args)
    return jnp.concatenate((out[0], out[1]), axis=1).reshape(T, 1, R, 256)


def solution(mesh):
    return jax.shard_map(
        per_device,
        mesh=mesh,
        in_specs=(P("frames", None, "rows", None), P(), P(), P(), P(), P(), P()),
        out_specs=P("frames", None, "rows", None),
        check_vma=False,
    )
```

```python
import functools
import math

import jax
import jax.numpy as jnp
import ml_dtypes
import numpy as np
from jax import lax
from jax.experimental import pallas as pl
from jax.experimental.pallas import tpu as pltpu
from jax.sharding import PartitionSpec as P

MESH = pl.DeviceIdType.MESH
BF16 = jnp.bfloat16
F32 = jnp.float32

NF = 8
T = 16
N = 128
R = 8
C = 16
O = 64
KB = 4
NB = N // KB
G = 16
NG = N // G
W = G + 2


def forward_table():
    k = np.arange(N)
    t = np.arange(N)
    angle = (2.0 * math.pi / N * (((k[:, None] - N // 2) * t[None, :]) % N)).astype(np.float32)
    scale = np.float32(1.0 / math.sqrt(N))
    re = (np.cos(angle) * scale).astype(ml_dtypes.bfloat16).astype(np.float32)
    im = (-np.sin(angle) * scale).astype(ml_dtypes.bfloat16).astype(np.float32)
    full = np.zeros((NF, 2, T, NG, 128), np.float32)
    for g in range(NG):
        for w in range(W):
            kk = g * G + w - 1
            if not 0 <= kk < N:
                continue
            a = re[kk].reshape(NF, T)
            b = im[kk].reshape(NF, T)
            for tap in range(3):
                lane = tap * 2 * W + w * 2
                full[:, 0, :, g, lane] = a
                full[:, 1, :, g, lane] = -b
                full[:, 0, :, g, lane + 1] = b
                full[:, 1, :, g, lane + 1] = a
    return full.reshape(NF * 2 * T, NG * 128).astype(ml_dtypes.bfloat16)


def inverse_table():
    k = np.arange(N)
    t = np.arange(N)
    angle = (2.0 * math.pi / N * (((k[:, None] - N // 2) * t[None, :]) % N)).astype(np.float32).T
    scale = np.float32(1.0 / math.sqrt(N))
    re = (np.cos(angle) * scale).reshape(NF, T, N)
    im = (np.sin(angle) * scale).reshape(NF, T, N)
    full = np.zeros((NF, 2, T, N, 2), np.float32)
    full[:, 0, :, :, 0] = re
    full[:, 0, :, :, 1] = -im
    full[:, 1, :, :, 0] = im
    full[:, 1, :, :, 1] = re
    return full.reshape(NF * 2 * T, N * 2).astype(ml_dtypes.bfloat16)


def place_table():
    full = np.zeros((G // KB, 128, KB, 32), np.float32)
    for q in range(G // KB):
        for j in range(KB):
            for a in range(3):
                for b in range(3):
                    for i in range(2):
                        full[q, b * 2 * W + (q * KB + j + a) * 2 + i, j, (a * 3 + b) * 2 + i] = 1
    return full.reshape(G // KB, 128, 128).astype(ml_dtypes.bfloat16)


def butterfly(parts):
    lane = lax.broadcasted_iota(jnp.int32, parts[0].shape, 1)
    for bit in range(3):
        step = 1 << bit
        upper = ((lane >> (4 + bit)) & 1) == 1
        out = list(parts)
        for i in range(8):
            if i & step:
                continue
            lo, hi = parts[i], parts[i + step]
            out[i] = jnp.where(upper, pltpu.roll(hi, 16 * step, 1), lo)
            out[i + step] = jnp.where(upper, hi, pltpu.roll(lo, 128 - 16 * step, 1))
        parts = out
    return parts


def kernel(
    n_rows,
    series,
    fwd,
    inv,
    place,
    lift,
    lift_bias,
    mix,
    mix_bias,
    proj,
    proj_bias,
    out,
    series_v,
    fwd_v,
    inv_v,
    place_v,
    lift_v,
    lift_bias_v,
    mix_v,
    mix_bias_v,
    proj_v,
    proj_bias_v,
    series_f,
    sent,
    got,
    xt,
    halo,
    spec,
    taps,
    ends,
    lift_m,
    mix_m,
    hid,
    upd,
    sent2,
    got2,
    load_sem,
    send_sem,
    recv_sem,
    halo_send_sem,
    halo_recv_sem,
    send2_sem,
    recv2_sem,
):
    f = lax.axis_index("frames")
    r = lax.axis_index("rows")
    above = lax.rem(r + n_rows - 1, n_rows)
    below = lax.rem(r + 1, n_rows)
    peers = [lax.rem(f + d, NF) for d in range(1, NF)]

    barrier = pltpu.get_barrier_semaphore()
    for p in peers:
        pl.semaphore_signal(barrier, inc=1, device_id={"frames": p}, device_id_type=MESH)
    for p in (above, below):
        pl.semaphore_signal(barrier, inc=1, device_id={"rows": p}, device_id_type=MESH)

    loads = [
        pltpu.make_async_copy(a, b, load_sem.at[i])
        for i, (a, b) in enumerate(
            (
                (series, series_v),
                (mix, mix_v),
                (lift, lift_v),
                (place, place_v),
                (fwd, fwd_v),
                (inv, inv_v),
                (lift_bias, lift_bias_v),
                (mix_bias, mix_bias_v),
                (proj, proj_v),
                (proj_bias, proj_bias_v),
            )
        )
    ]
    for c in loads:
        c.start()

    loads[0].wait()
    for ri in range(2):
        series_f[ri] = series_v[:, 0, :, ri * 128 : ri * 128 + 128].astype(F32).reshape(T * R, 128)
    for ri in range(2):
        parts = [series_f[ri, pl.ds(i, T, stride=R), :] for i in range(R)]
        for i, part in enumerate(butterfly(parts)):
            sent[i, ri * T : ri * T + T, :] = part.astype(BF16)

    pl.semaphore_wait(barrier, NF + 1)
    first = [
        pltpu.make_async_remote_copy(
            src_ref=sent.at[p],
            dst_ref=got.at[f],
            send_sem=send_sem.at[i],
            recv_sem=recv_sem.at[i],
            device_id={"frames": p},
            device_id_type=MESH,
        )
        for i, p in enumerate(peers)
    ]
    for c in first:
        c.start()
    got[f] = sent[f]

    for c in loads[1:]:
        c.wait()
    taps[...] = jnp.zeros(taps.shape, F32)
    for a in range(3):
        for b in range(3):
            taps[(a * 3 + b) * 2 : (a * 3 + b) * 2 + 2, :O] = lift_v[a, b].astype(F32)
    left = taps[...]
    right = pltpu.roll(left, O, 1)
    none = jnp.zeros_like(left)
    lift4 = jnp.concatenate(
        [jnp.concatenate(p, axis=1) for p in ((left, none), (right, none), (none, left), (none, right))],
        axis=0,
    ).astype(BF16)
    for q in range(G // KB):
        lift_m[:, q * 256 : q * 256 + 256] = jnp.dot(
            place_v[q], lift4, preferred_element_type=F32
        ).astype(BF16)
    for k in range(KB):
        ends[k * 2 : k * 2 + 2, :] = proj_v[...].astype(F32)
    proj4 = jnp.concatenate([ends[...]] * KB, axis=1)
    proj4 = jnp.where(
        lax.broadcasted_iota(jnp.int32, proj4.shape, 0) // 2
        == lax.broadcasted_iota(jnp.int32, proj4.shape, 1) // O,
        proj4,
        0.0,
    ).astype(BF16)
    lift_bias4 = jnp.concatenate([lift_bias_v[...]] * KB, axis=1)
    mix_bias4 = jnp.concatenate([mix_bias_v[...]] * KB, axis=1)
    proj_bias4 = jnp.where(
        lax.broadcasted_iota(jnp.int32, (8, 128), 0) % 2 == 0,
        jnp.broadcast_to(proj_bias_v[:, :1], (8, 128)),
        jnp.broadcast_to(proj_bias_v[:, 1:], (8, 128)),
    )
    zero = jnp.zeros((O, O), BF16)
    for b in range(3):
        t0, t1, t2 = (mix_v[a, b] for a in range(3))
        rows = (
            (t1, t0, zero, zero),
            (t2, t1, t0, zero),
            (zero, t2, t1, t0),
            (zero, zero, t2, t1),
        )
        for j, row in enumerate(rows):
            mix_m[b * 256 + j * O : b * 256 + j * O + O, :] = jnp.concatenate(row, axis=1)
        mix_m[768 + b * 128 : 768 + b * 128 + O, :] = jnp.concatenate((zero, zero, zero, t2), axis=1)
        mix_m[768 + b * 128 + O : 768 + b * 128 + 128, :] = jnp.concatenate((t0, zero, zero, zero), axis=1)
    hid[0] = jnp.zeros(hid.shape[1:], BF16)
    hid[NB + 1] = jnp.zeros(hid.shape[1:], BF16)

    for c in first:
        c.wait_recv()
    xt[...] = got[...].reshape(256, 128).T

    halos = [
        pltpu.make_async_remote_copy(
            src_ref=xt.at[pl.ds(lo, 2 * C)],
            dst_ref=halo.at[i],
            send_sem=halo_send_sem.at[i],
            recv_sem=halo_recv_sem.at[i],
            device_id={"rows": p},
            device_id_type=MESH,
        )
        for i, (lo, p) in enumerate(((6 * C, below), (0, above)))
    ]
    for c in halos:
        c.start()

    own = jnp.dot(xt[...], fwd_v[...], preferred_element_type=F32).astype(BF16)
    for g in range(NG):
        spec[g, 2 * C : 10 * C, :] = own[:, g * 128 : g * 128 + 128]

    def gather(g, lo, size):
        lane = lax.broadcasted_iota(jnp.int32, (size, 128), 1)
        rows = [spec[g, lo + b * C : lo + b * C + size, :] for b in range(3)]
        return jnp.where(lane < 2 * W, rows[0], jnp.where(lane < 4 * W, rows[1], rows[2]))

    def lifted(patch):
        return [
            jnp.maximum(
                jnp.dot(patch, lift_m[:, q * 256 : q * 256 + 256], preferred_element_type=F32)
                + lift_bias4,
                0.0,
            )
            for q in range(G // KB)
        ]

    for g in range(NG):
        for q, h in enumerate(lifted(gather(g, 2 * C, 6 * C))):
            hid[g * KB + q + 1, 2 * C : 8 * C, :] = h.astype(BF16)

    for c in halos:
        c.wait_recv()
    top = jnp.where(r > 0, halo[0], jnp.zeros_like(halo[0]))
    bottom = jnp.where(r < n_rows - 1, halo[1], jnp.zeros_like(halo[1]))
    outer = jnp.dot(
        jnp.concatenate((top, bottom), axis=0), fwd_v[...], preferred_element_type=F32
    ).astype(BF16)
    for g in range(NG):
        spec[g, : 2 * C, :] = outer[: 2 * C, g * 128 : g * 128 + 128]
        spec[g, 10 * C :, :] = outer[2 * C :, g * 128 : g * 128 + 128]

    row = lax.broadcasted_iota(jnp.int32, (4 * C, 256), 0)
    keep = ((row >= C) | (r > 0)) & ((row < 3 * C) | (r < n_rows - 1))
    for g in range(NG):
        patch = jnp.concatenate((gather(g, 0, 2 * C), gather(g, 8 * C, 2 * C)), axis=0)
        for q, h in enumerate(lifted(patch)):
            h = jnp.where(keep, h, 0.0).astype(BF16)
            hid[g * KB + q + 1, : 2 * C, :] = h[: 2 * C]
            hid[g * KB + q + 1, 8 * C :, :] = h[2 * C :]

    lane = lax.broadcasted_iota(jnp.int32, (8 * C, 128), 1)
    rows = []
    for kb in range(1, NB + 1):
        taps_b = [pl.ds(b * C, 8 * C) for b in range(3)]
        main = [hid[kb, at, :] for at in taps_b]
        edge = [jnp.where(lane < O, hid[kb + 1, at, :128], hid[kb - 1, at, 128:]) for at in taps_b]
        rows.append(jnp.concatenate(main + edge, axis=1))
    total = jnp.dot(jnp.concatenate(rows, axis=0), mix_m[...], preferred_element_type=F32)
    mixed = jnp.maximum(total + mix_bias4, 0.0).astype(BF16)
    u = lax.dot_general(proj4, mixed, (((1,), (1,)), ((), ())), preferred_element_type=F32)
    for kb in range(NB):
        upd[kb * 8 : kb * 8 + 8, :] = u[:, kb * 128 : kb * 128 + 128] + proj_bias4

    back = jnp.dot(inv_v[...], upd[...].astype(BF16), preferred_element_type=F32)
    sent2[...] = back.astype(BF16).reshape(NF, 2 * T, 128)

    second = [
        pltpu.make_async_remote_copy(
            src_ref=sent2.at[p],
            dst_ref=got2.at[f],
            send_sem=send2_sem.at[i],
            recv_sem=recv2_sem.at[i],
            device_id={"frames": p},
            device_id_type=MESH,
        )
        for i, p in enumerate(peers)
    ]
    for c in second:
        c.start()
    got2[f] = sent2[f]
    for c in first + halos:
        c.wait_send()
    for c in second:
        c.wait_recv()
    for ri in range(2):
        parts = [got2[i, ri * T : ri * T + T, :].astype(F32) for i in range(NF)]
        for i, part in enumerate(butterfly(parts)):
            at = (ri, pl.ds(i, T, stride=R), slice(None))
            out[at] = part + series_f[at]
    for c in second:
        c.wait_send()


def per_device(series, lift_weight, lift_bias, mix_weight, mix_bias, proj_weight, proj_bias):
    n_rows = lax.axis_size("rows")
    args = (
        series,
        jnp.asarray(forward_table()),
        jnp.asarray(inverse_table()),
        jnp.asarray(place_table()),
        lift_weight,
        lift_bias[None],
        mix_weight,
        mix_bias[None],
        proj_weight.T,
        proj_bias[None],
    )
    scratch = [pltpu.VMEM(a.shape, a.dtype) for a in args]
    out = pl.pallas_call(
        functools.partial(kernel, n_rows),
        out_shape=jax.ShapeDtypeStruct((2, T * R, 128), F32),
        in_specs=[pl.BlockSpec(memory_space=pltpu.HBM)] * len(args),
        out_specs=pl.BlockSpec(memory_space=pltpu.VMEM),
        scratch_shapes=scratch
        + [
            pltpu.VMEM((2, T * R, 128), F32),
            pltpu.VMEM((NF, 2 * T, 128), BF16),
            pltpu.VMEM((NF, 2 * T, 128), BF16),
            pltpu.VMEM((R * C, 256), BF16),
            pltpu.VMEM((2, 2 * C, 256), BF16),
            pltpu.VMEM((NG, 12 * C, 128), BF16),
            pltpu.VMEM((32, 128), F32),
            pltpu.VMEM((8, O), F32),
            pltpu.VMEM((128, G * O), BF16),
            pltpu.VMEM((1152, 256), BF16),
            pltpu.VMEM((NB + 2, 10 * C, 256), BF16),
            pltpu.VMEM((2 * N, 128), F32),
            pltpu.VMEM((NF, 2 * T, 128), BF16),
            pltpu.VMEM((NF, 2 * T, 128), BF16),
            pltpu.SemaphoreType.DMA((len(args),)),
            pltpu.SemaphoreType.DMA((NF - 1,)),
            pltpu.SemaphoreType.DMA((NF - 1,)),
            pltpu.SemaphoreType.DMA((2,)),
            pltpu.SemaphoreType.DMA((2,)),
            pltpu.SemaphoreType.DMA((NF - 1,)),
            pltpu.SemaphoreType.DMA((NF - 1,)),
        ],
        compiler_params=pltpu.CompilerParams(
            collective_id=0, has_side_effects=True, vmem_limit_bytes=58 * 1024 * 1024
        ),
    )(*args)
    return jnp.concatenate((out[0], out[1]), axis=1).reshape(T, 1, R, 256)


def solution(mesh):
    return jax.shard_map(
        per_device,
        mesh=mesh,
        in_specs=(P("frames", None, "rows", None), P(), P(), P(), P(), P(), P()),
        out_specs=P("frames", None, "rows", None),
        check_vma=False,
    )
```

```python
import functools
import math

import jax
import jax.numpy as jnp
import ml_dtypes
import numpy as np
from jax import lax
from jax.experimental import pallas as pl
from jax.experimental.pallas import tpu as pltpu
from jax.sharding import PartitionSpec as P

MESH = pl.DeviceIdType.MESH
BF16 = jnp.bfloat16
F32 = jnp.float32

NF = 8
T = 16
N = 128
R = 8
C = 16
O = 64
KB = 4
NB = N // KB
G = 16
NG = N // G
W = G + 2


def forward_table():
    k = np.arange(N)
    t = np.arange(N)
    angle = (2.0 * math.pi / N * (((k[:, None] - N // 2) * t[None, :]) % N)).astype(np.float32)
    scale = np.float32(1.0 / math.sqrt(N))
    re = (np.cos(angle) * scale).astype(ml_dtypes.bfloat16).astype(np.float32)
    im = (-np.sin(angle) * scale).astype(ml_dtypes.bfloat16).astype(np.float32)
    full = np.zeros((NF, 2, T, NG, 128), np.float32)
    for g in range(NG):
        for w in range(W):
            kk = g * G + w - 1
            if not 0 <= kk < N:
                continue
            a = re[kk].reshape(NF, T)
            b = im[kk].reshape(NF, T)
            for tap in range(3):
                lane = tap * 2 * W + w * 2
                full[:, 0, :, g, lane] = a
                full[:, 1, :, g, lane] = -b
                full[:, 0, :, g, lane + 1] = b
                full[:, 1, :, g, lane + 1] = a
    return full.reshape(NF * 2 * T, NG * 128).astype(ml_dtypes.bfloat16)


def inverse_table():
    k = np.arange(N)
    t = np.arange(N)
    angle = (2.0 * math.pi / N * (((k[:, None] - N // 2) * t[None, :]) % N)).astype(np.float32).T
    scale = np.float32(1.0 / math.sqrt(N))
    re = (np.cos(angle) * scale).reshape(NF, T, N)
    im = (np.sin(angle) * scale).reshape(NF, T, N)
    full = np.zeros((NF, 2, T, N, 2), np.float32)
    full[:, 0, :, :, 0] = re
    full[:, 0, :, :, 1] = -im
    full[:, 1, :, :, 0] = im
    full[:, 1, :, :, 1] = re
    return full.reshape(NF * 2 * T, N * 2).astype(ml_dtypes.bfloat16)


def place_table():
    full = np.zeros((G // KB, 128, KB, 32), np.float32)
    for q in range(G // KB):
        for j in range(KB):
            for a in range(3):
                for b in range(3):
                    for i in range(2):
                        full[q, b * 2 * W + (q * KB + j + a) * 2 + i, j, (a * 3 + b) * 2 + i] = 1
    return full.reshape(G // KB, 128, 128).astype(ml_dtypes.bfloat16)


PARTNERS = (5, 7, 3, 1, 4, 6, 2)


def partner(f, m):
    for bit in range(3):
        if m >> bit & 1:
            f = f + (1 << bit) * (1 - 2 * (f // (1 << bit) % 2))
    return f


def butterfly(parts):
    lane = lax.broadcasted_iota(jnp.int32, parts[0].shape, 1)
    for bit in range(3):
        step = 1 << bit
        upper = ((lane >> (4 + bit)) & 1) == 1
        out = list(parts)
        for i in range(8):
            if i & step:
                continue
            lo, hi = parts[i], parts[i + step]
            out[i] = jnp.where(upper, pltpu.roll(hi, 16 * step, 1), lo)
            out[i + step] = jnp.where(upper, hi, pltpu.roll(lo, 128 - 16 * step, 1))
        parts = out
    return parts


def kernel(
    n_rows,
    series,
    fwd,
    inv,
    place,
    lift,
    lift_bias,
    mix,
    mix_bias,
    proj,
    proj_bias,
    out,
    series_v,
    fwd_v,
    inv_v,
    place_v,
    lift_v,
    lift_bias_v,
    mix_v,
    mix_bias_v,
    proj_v,
    proj_bias_v,
    series_f,
    sent,
    got,
    xt,
    halo,
    spec,
    taps,
    ends,
    lift_m,
    mix_m,
    hid,
    mixed,
    sent2,
    got2,
    load_sem,
    send_sem,
    recv_sem,
    halo_send_sem,
    halo_recv_sem,
    send2_sem,
    recv2_sem,
):
    f = lax.axis_index("frames")
    r = lax.axis_index("rows")
    above = lax.rem(r + n_rows - 1, n_rows)
    below = lax.rem(r + 1, n_rows)
    has_above = r > 0
    has_below = r < n_rows - 1
    peers = [partner(f, m) for m in PARTNERS]

    barrier = pltpu.get_barrier_semaphore()
    for p in peers:
        pl.semaphore_signal(barrier, inc=1, device_id={"frames": p}, device_id_type=MESH)

    @pl.when(has_above)
    def _():
        pl.semaphore_signal(barrier, inc=1, device_id={"rows": above}, device_id_type=MESH)

    @pl.when(has_below)
    def _():
        pl.semaphore_signal(barrier, inc=1, device_id={"rows": below}, device_id_type=MESH)

    loads = [
        pltpu.make_async_copy(a, b, load_sem.at[i])
        for i, (a, b) in enumerate(
            (
                (series, series_v),
                (mix, mix_v),
                (lift, lift_v),
                (place, place_v),
                (fwd, fwd_v),
                (inv, inv_v),
                (lift_bias, lift_bias_v),
                (mix_bias, mix_bias_v),
                (proj, proj_v),
                (proj_bias, proj_bias_v),
            )
        )
    ]
    for c in loads:
        c.start()

    loads[0].wait()
    for ri in range(2):
        series_f[ri] = series_v[:, 0, :, ri * 128 : ri * 128 + 128].astype(F32).reshape(T * R, 128)
    for ri in range(2):
        parts = [series_f[ri, pl.ds(i, T, stride=R), :] for i in range(R)]
        for i, part in enumerate(butterfly(parts)):
            sent[i, ri * T : ri * T + T, :] = part.astype(BF16)

    neighbours = jnp.where(has_above, 1, 0) + jnp.where(has_below, 1, 0)
    pl.semaphore_wait(barrier, NF - 1 + neighbours)
    first = [
        pltpu.make_async_remote_copy(
            src_ref=sent.at[p],
            dst_ref=got.at[f],
            send_sem=send_sem.at[i],
            recv_sem=recv_sem.at[i],
            device_id={"frames": p},
            device_id_type=MESH,
        )
        for i, p in enumerate(peers)
    ]
    for c in first:
        c.start()
    got[f] = sent[f]

    for c in loads[1:]:
        c.wait()
    taps[...] = jnp.zeros(taps.shape, F32)
    for a in range(3):
        for b in range(3):
            taps[(a * 3 + b) * 2 : (a * 3 + b) * 2 + 2, :O] = lift_v[a, b].astype(F32)
    left = taps[...]
    right = pltpu.roll(left, O, 1)
    none = jnp.zeros_like(left)
    lift4 = jnp.concatenate(
        [jnp.concatenate(p, axis=1) for p in ((left, none), (right, none), (none, left), (none, right))],
        axis=0,
    ).astype(BF16)
    for q in range(G // KB):
        lift_m[:, q * 256 : q * 256 + 256] = jnp.dot(
            place_v[q], lift4, preferred_element_type=F32
        ).astype(BF16)
    for k in range(KB):
        ends[k * 2 : k * 2 + 2, :] = proj_v[...].astype(F32)
    proj4 = jnp.concatenate([ends[...]] * KB, axis=1)
    proj4 = jnp.where(
        lax.broadcasted_iota(jnp.int32, proj4.shape, 0) // 2
        == lax.broadcasted_iota(jnp.int32, proj4.shape, 1) // O,
        proj4,
        0.0,
    ).astype(BF16)
    lift_bias4 = jnp.concatenate([lift_bias_v[...]] * KB, axis=1)
    mix_bias4 = jnp.concatenate([mix_bias_v[...]] * KB, axis=1)
    proj_bias4 = jnp.where(
        lax.broadcasted_iota(jnp.int32, (8, 128), 0) % 2 == 0,
        jnp.broadcast_to(proj_bias_v[:, :1], (8, 128)),
        jnp.broadcast_to(proj_bias_v[:, 1:], (8, 128)),
    )
    zero = jnp.zeros((O, O), BF16)
    for b in range(3):
        t0, t1, t2 = (mix_v[a, b] for a in range(3))
        rows = (
            (t1, t0, zero, zero),
            (t2, t1, t0, zero),
            (zero, t2, t1, t0),
            (zero, zero, t2, t1),
        )
        for j, row in enumerate(rows):
            mix_m[b * 256 + j * O : b * 256 + j * O + O, :] = jnp.concatenate(row, axis=1)
        mix_m[768 + b * 128 : 768 + b * 128 + O, :] = jnp.concatenate((zero, zero, zero, t2), axis=1)
        mix_m[768 + b * 128 + O : 768 + b * 128 + 128, :] = jnp.concatenate((t0, zero, zero, zero), axis=1)
    hid[0] = jnp.zeros(hid.shape[1:], BF16)
    hid[NB + 1] = jnp.zeros(hid.shape[1:], BF16)

    for c in first:
        c.wait_recv()
    xt[...] = got[...].reshape(256, 128).T

    halos = [
        pltpu.make_async_remote_copy(
            src_ref=xt.at[pl.ds(lo, 2 * C)],
            dst_ref=halo.at[i],
            send_sem=halo_send_sem.at[i],
            recv_sem=halo_recv_sem.at[i],
            device_id={"rows": p},
            device_id_type=MESH,
        )
        for i, (lo, p) in enumerate(((6 * C, below), (0, above)))
    ]
    down, up = halos

    @pl.when(has_below)
    def _():
        down.start()

    @pl.when(has_above)
    def _():
        up.start()

    @pl.when(r == 0)
    def _():
        halo[0] = jnp.zeros(halo.shape[1:], BF16)

    @pl.when(r == n_rows - 1)
    def _():
        halo[1] = jnp.zeros(halo.shape[1:], BF16)

    own = jnp.dot(xt[...], fwd_v[...], preferred_element_type=F32).astype(BF16)
    for g in range(NG):
        spec[g, 2 * C : 10 * C, :] = own[:, g * 128 : g * 128 + 128]

    lane = lax.broadcasted_iota(jnp.int32, (10 * C, 128), 1)

    def gather(g, lo, size):
        rows = [spec[g, lo + b * C : lo + b * C + size, :] for b in range(3)]
        at = lane[:size]
        return jnp.where(at < 2 * W, rows[0], jnp.where(at < 4 * W, rows[1], rows[2]))

    def lift_rows(parts):
        size = sum(n for _, n in parts)
        patch = jnp.concatenate([gather(g, lo, n) for g in range(NG) for lo, n in parts], axis=0)
        for q in range(G // KB):
            h = jnp.dot(patch, lift_m[:, q * 256 : q * 256 + 256], preferred_element_type=F32)
            h = jnp.maximum(h + lift_bias4, 0.0).astype(BF16)
            for g in range(NG):
                at = g * size
                for lo, n in parts:
                    hid[g * KB + q + 1, lo : lo + n, :] = h[at : at + n]
                    at += n

    def mix_rows(parts):
        rows = []
        for kb in range(1, NB + 1):
            for lo, n in parts:
                at = [pl.ds(lo + b * C, n) for b in range(3)]
                main = [hid[kb, i, :] for i in at]
                edge = [jnp.where(lane[:n] < O, hid[kb + 1, i, :128], hid[kb - 1, i, 128:]) for i in at]
                rows.append(jnp.concatenate(main + edge, axis=1))
        total = jnp.dot(jnp.concatenate(rows, axis=0), mix_m[...], preferred_element_type=F32)
        total = jnp.maximum(total + mix_bias4, 0.0).astype(BF16)
        at = 0
        for kb in range(NB):
            for lo, n in parts:
                mixed[kb, lo : lo + n, :] = total[at : at + n]
                at += n

    lift_rows([(2 * C, 6 * C)])
    mix_rows([(2 * C, 4 * C)])

    @pl.when(has_above)
    def _():
        down.wait_recv()

    @pl.when(has_below)
    def _():
        up.wait_recv()

    outer = jnp.dot(
        halo[...].reshape(4 * C, 256), fwd_v[...], preferred_element_type=F32
    ).astype(BF16)
    for g in range(NG):
        spec[g, : 2 * C, :] = outer[: 2 * C, g * 128 : g * 128 + 128]
        spec[g, 10 * C :, :] = outer[2 * C :, g * 128 : g * 128 + 128]
    lift_rows([(0, 2 * C), (8 * C, 2 * C)])

    @pl.when(r == 0)
    def _():
        hid[:, :C, :] = jnp.zeros((NB + 2, C, 256), BF16)

    @pl.when(r == n_rows - 1)
    def _():
        hid[:, 9 * C :, :] = jnp.zeros((NB + 2, C, 256), BF16)

    mix_rows([(0, 2 * C), (6 * C, 2 * C)])
    u = lax.dot_general(
        proj4,
        mixed[...].reshape(NB * 8 * C, 256),
        (((1,), (1,)), ((), ())),
        preferred_element_type=F32,
    )
    update = jnp.concatenate(
        [u[:, kb * 128 : kb * 128 + 128] + proj_bias4 for kb in range(NB)], axis=0
    ).astype(BF16)
    back = jnp.dot(inv_v[...], update, preferred_element_type=F32)
    sent2[...] = back.astype(BF16).reshape(NF, 2 * T, 128)

    second = [
        pltpu.make_async_remote_copy(
            src_ref=sent2.at[p],
            dst_ref=got2.at[f],
            send_sem=send2_sem.at[i],
            recv_sem=recv2_sem.at[i],
            device_id={"frames": p},
            device_id_type=MESH,
        )
        for i, p in enumerate(peers)
    ]
    for c in second:
        c.start()
    got2[f] = sent2[f]
    for c in second:
        c.wait_recv()
    for ri in range(2):
        parts = [got2[i, ri * T : ri * T + T, :].astype(F32) for i in range(NF)]
        for i, part in enumerate(butterfly(parts)):
            at = (ri, pl.ds(i, T, stride=R), slice(None))
            out[at] = part + series_f[at]
    for c in first + second:
        c.wait_send()

    @pl.when(has_below)
    def _():
        down.wait_send()

    @pl.when(has_above)
    def _():
        up.wait_send()


def per_device(series, lift_weight, lift_bias, mix_weight, mix_bias, proj_weight, proj_bias):
    n_rows = lax.axis_size("rows")
    args = (
        series,
        jnp.asarray(forward_table()),
        jnp.asarray(inverse_table()),
        jnp.asarray(place_table()),
        lift_weight,
        lift_bias[None],
        mix_weight,
        mix_bias[None],
        proj_weight.T,
        proj_bias[None],
    )
    scratch = [pltpu.VMEM(a.shape, a.dtype) for a in args]
    out = pl.pallas_call(
        functools.partial(kernel, n_rows),
        out_shape=pltpu.VMEM((2, T * R, 128), F32),
        in_specs=[pl.BlockSpec(memory_space=pltpu.HBM)] * len(args),
        out_specs=pl.BlockSpec(memory_space=pltpu.VMEM),
        scratch_shapes=scratch
        + [
            pltpu.VMEM((2, T * R, 128), F32),
            pltpu.VMEM((NF, 2 * T, 128), BF16),
            pltpu.VMEM((NF, 2 * T, 128), BF16),
            pltpu.VMEM((R * C, 256), BF16),
            pltpu.VMEM((2, 2 * C, 256), BF16),
            pltpu.VMEM((NG, 12 * C, 128), BF16),
            pltpu.VMEM((32, 128), F32),
            pltpu.VMEM((8, O), F32),
            pltpu.VMEM((128, G * O), BF16),
            pltpu.VMEM((1152, 256), BF16),
            pltpu.VMEM((NB + 2, 10 * C, 256), BF16),
            pltpu.VMEM((NB, R * C, 256), BF16),
            pltpu.VMEM((NF, 2 * T, 128), BF16),
            pltpu.VMEM((NF, 2 * T, 128), BF16),
            pltpu.SemaphoreType.DMA((len(args),)),
            pltpu.SemaphoreType.DMA((NF - 1,)),
            pltpu.SemaphoreType.DMA((NF - 1,)),
            pltpu.SemaphoreType.DMA((2,)),
            pltpu.SemaphoreType.DMA((2,)),
            pltpu.SemaphoreType.DMA((NF - 1,)),
            pltpu.SemaphoreType.DMA((NF - 1,)),
        ],
        compiler_params=pltpu.CompilerParams(
            collective_id=0, has_side_effects=True, vmem_limit_bytes=56 * 1024 * 1024
        ),
    )(*args)
    return jnp.concatenate((out[0], out[1]), axis=1).reshape(T, 1, R, 256)


def solution(mesh):
    return jax.shard_map(
        per_device,
        mesh=mesh,
        in_specs=(P("frames", None, "rows", None), P(), P(), P(), P(), P(), P()),
        out_specs=P("frames", None, "rows", None),
        check_vma=False,
    )
```

```python
import functools
import math

import jax
import jax.numpy as jnp
import ml_dtypes
import numpy as np
from jax import lax
from jax.experimental import pallas as pl
from jax.experimental.pallas import tpu as pltpu
from jax.sharding import PartitionSpec as P

MESH = pl.DeviceIdType.MESH
BF16 = jnp.bfloat16
F32 = jnp.float32

NF = 8
T = 16
N = 128
R = 8
C = 16
O = 64
KB = 4
NB = N // KB
G = 16
NG = N // G
W = G + 2


def forward_table():
    k = np.arange(N)
    t = np.arange(N)
    angle = (2.0 * math.pi / N * (((k[:, None] - N // 2) * t[None, :]) % N)).astype(np.float32)
    scale = np.float32(1.0 / math.sqrt(N))
    re = (np.cos(angle) * scale).astype(ml_dtypes.bfloat16).astype(np.float32)
    im = (-np.sin(angle) * scale).astype(ml_dtypes.bfloat16).astype(np.float32)
    full = np.zeros((NF, 2, T, NG, 128), np.float32)
    for g in range(NG):
        for w in range(W):
            kk = g * G + w - 1
            if not 0 <= kk < N:
                continue
            a = re[kk].reshape(NF, T)
            b = im[kk].reshape(NF, T)
            for tap in range(3):
                lane = tap * 2 * W + w * 2
                full[:, 0, :, g, lane] = a
                full[:, 1, :, g, lane] = -b
                full[:, 0, :, g, lane + 1] = b
                full[:, 1, :, g, lane + 1] = a
    return full.reshape(NF * 2 * T, NG * 128).astype(ml_dtypes.bfloat16)


def inverse_table():
    k = np.arange(N)
    t = np.arange(N)
    angle = (2.0 * math.pi / N * (((k[:, None] - N // 2) * t[None, :]) % N)).astype(np.float32).T
    scale = np.float32(1.0 / math.sqrt(N))
    re = (np.cos(angle) * scale).reshape(NF, T, N)
    im = (np.sin(angle) * scale).reshape(NF, T, N)
    full = np.zeros((NF, 2, T, N, 2), np.float32)
    full[:, 0, :, :, 0] = re
    full[:, 0, :, :, 1] = -im
    full[:, 1, :, :, 0] = im
    full[:, 1, :, :, 1] = re
    return full.reshape(NF * 2 * T, N * 2).astype(ml_dtypes.bfloat16)


def place_table():
    full = np.zeros((G // KB, 128, KB, 32), np.float32)
    for q in range(G // KB):
        for j in range(KB):
            for a in range(3):
                for b in range(3):
                    for i in range(2):
                        full[q, b * 2 * W + (q * KB + j + a) * 2 + i, j, (a * 3 + b) * 2 + i] = 1
    return full.reshape(G // KB, 128, 128).astype(ml_dtypes.bfloat16)


PARTNERS = (5, 7, 3, 1, 4, 6, 2)


def partner(f, m):
    for bit in range(3):
        if m >> bit & 1:
            f = f + (1 << bit) * (1 - 2 * (f // (1 << bit) % 2))
    return f


def butterfly(parts):
    lane = lax.broadcasted_iota(jnp.int32, parts[0].shape, 1)
    for bit in range(3):
        step = 1 << bit
        upper = ((lane >> (4 + bit)) & 1) == 1
        out = list(parts)
        for i in range(8):
            if i & step:
                continue
            lo, hi = parts[i], parts[i + step]
            out[i] = jnp.where(upper, pltpu.roll(hi, 16 * step, 1), lo)
            out[i + step] = jnp.where(upper, hi, pltpu.roll(lo, 128 - 16 * step, 1))
        parts = out
    return parts


def kernel(
    n_rows,
    series,
    fwd,
    inv,
    place,
    lift,
    lift_bias,
    mix,
    mix_bias,
    proj,
    proj_bias,
    out,
    series_v,
    fwd_v,
    inv_v,
    place_v,
    lift_v,
    lift_bias_v,
    mix_v,
    mix_bias_v,
    proj_v,
    proj_bias_v,
    series_f,
    sent,
    got,
    xt,
    halo,
    spec,
    taps,
    ends,
    lift_m,
    mix_m,
    hid,
    mixed,
    sent2,
    got2,
    load_sem,
    send_sem,
    recv_sem,
    halo_send_sem,
    halo_recv_sem,
    send2_sem,
    recv2_sem,
):
    f = lax.axis_index("frames")
    r = lax.axis_index("rows")
    above = lax.rem(r + n_rows - 1, n_rows)
    below = lax.rem(r + 1, n_rows)
    has_above = r > 0
    has_below = r < n_rows - 1
    peers = [partner(f, m) for m in PARTNERS]

    barrier = pltpu.get_barrier_semaphore()
    for p in peers:
        pl.semaphore_signal(barrier, inc=1, device_id={"frames": p}, device_id_type=MESH)

    @pl.when(has_above)
    def _():
        pl.semaphore_signal(barrier, inc=1, device_id={"rows": above}, device_id_type=MESH)

    @pl.when(has_below)
    def _():
        pl.semaphore_signal(barrier, inc=1, device_id={"rows": below}, device_id_type=MESH)

    loads = [
        pltpu.make_async_copy(a, b, load_sem.at[i])
        for i, (a, b) in enumerate(
            (
                (series, series_v),
                (mix, mix_v),
                (lift, lift_v),
                (place, place_v),
                (fwd, fwd_v),
                (inv, inv_v),
                (lift_bias, lift_bias_v),
                (mix_bias, mix_bias_v),
                (proj, proj_v),
                (proj_bias, proj_bias_v),
            )
        )
    ]
    for c in loads:
        c.start()

    loads[0].wait()
    for ri in range(2):
        series_f[ri] = series_v[:, 0, :, ri * 128 : ri * 128 + 128].astype(F32).reshape(T * R, 128)
    for ri in range(2):
        parts = [series_f[ri, pl.ds(i, T, stride=R), :] for i in range(R)]
        for i, part in enumerate(butterfly(parts)):
            sent[i, ri * T : ri * T + T, :] = part.astype(BF16)

    neighbours = jnp.where(has_above, 1, 0) + jnp.where(has_below, 1, 0)
    pl.semaphore_wait(barrier, NF - 1 + neighbours)
    first = [
        pltpu.make_async_remote_copy(
            src_ref=sent.at[p],
            dst_ref=got.at[f],
            send_sem=send_sem.at[i],
            recv_sem=recv_sem.at[i],
            device_id={"frames": p},
            device_id_type=MESH,
        )
        for i, p in enumerate(peers)
    ]
    for c in first:
        c.start()
    got[f] = sent[f]

    for c in loads[1:]:
        c.wait()
    taps[...] = jnp.zeros(taps.shape, F32)
    for a in range(3):
        for b in range(3):
            taps[(a * 3 + b) * 2 : (a * 3 + b) * 2 + 2, :O] = lift_v[a, b].astype(F32)
    left = taps[...]
    right = pltpu.roll(left, O, 1)
    none = jnp.zeros_like(left)
    lift4 = jnp.concatenate(
        [jnp.concatenate(p, axis=1) for p in ((left, none), (right, none), (none, left), (none, right))],
        axis=0,
    ).astype(BF16)
    for q in range(G // KB):
        lift_m[:, q * 256 : q * 256 + 256] = jnp.dot(
            place_v[q], lift4, preferred_element_type=F32
        ).astype(BF16)
    for k in range(KB):
        ends[k * 2 : k * 2 + 2, :] = proj_v[...].astype(F32)
    proj4 = jnp.concatenate([ends[...]] * KB, axis=1)
    proj4 = jnp.where(
        lax.broadcasted_iota(jnp.int32, proj4.shape, 0) // 2
        == lax.broadcasted_iota(jnp.int32, proj4.shape, 1) // O,
        proj4,
        0.0,
    ).astype(BF16)
    lift_bias4 = jnp.concatenate([lift_bias_v[...]] * KB, axis=1)
    mix_bias4 = jnp.concatenate([mix_bias_v[...]] * KB, axis=1)
    proj_bias4 = jnp.where(
        lax.broadcasted_iota(jnp.int32, (8, 128), 0) % 2 == 0,
        jnp.broadcast_to(proj_bias_v[:, :1], (8, 128)),
        jnp.broadcast_to(proj_bias_v[:, 1:], (8, 128)),
    )
    zero = jnp.zeros((O, O), BF16)
    for b in range(3):
        t0, t1, t2 = (mix_v[a, b] for a in range(3))
        rows = (
            (t1, t0, zero, zero),
            (t2, t1, t0, zero),
            (zero, t2, t1, t0),
            (zero, zero, t2, t1),
        )
        for j, row in enumerate(rows):
            mix_m[b * 256 + j * O : b * 256 + j * O + O, :] = jnp.concatenate(row, axis=1)
        mix_m[768 + b * 128 : 768 + b * 128 + O, :] = jnp.concatenate((zero, zero, zero, t2), axis=1)
        mix_m[768 + b * 128 + O : 768 + b * 128 + 128, :] = jnp.concatenate((t0, zero, zero, zero), axis=1)
    hid[0] = jnp.zeros(hid.shape[1:], BF16)
    hid[NB + 1] = jnp.zeros(hid.shape[1:], BF16)

    for c in first:
        c.wait_recv()
    xt[...] = got[...].reshape(256, 128).T

    halos = [
        pltpu.make_async_remote_copy(
            src_ref=xt.at[pl.ds(lo, 2 * C)],
            dst_ref=halo.at[i],
            send_sem=halo_send_sem.at[i],
            recv_sem=halo_recv_sem.at[i],
            device_id={"rows": p},
            device_id_type=MESH,
        )
        for i, (lo, p) in enumerate(((6 * C, below), (0, above)))
    ]
    down, up = halos

    @pl.when(has_below)
    def _():
        down.start()

    @pl.when(has_above)
    def _():
        up.start()

    @pl.when(r == 0)
    def _():
        halo[0] = jnp.zeros(halo.shape[1:], BF16)

    @pl.when(r == n_rows - 1)
    def _():
        halo[1] = jnp.zeros(halo.shape[1:], BF16)

    own = jnp.dot(xt[...], fwd_v[...], preferred_element_type=F32).astype(BF16)
    for g in range(NG):
        spec[g, 2 * C : 10 * C, :] = own[:, g * 128 : g * 128 + 128]

    lane = lax.broadcasted_iota(jnp.int32, (10 * C, 128), 1)

    def gather(g, lo, size):
        rows = [spec[g, lo + b * C : lo + b * C + size, :] for b in range(3)]
        at = lane[:size]
        return jnp.where(at < 2 * W, rows[0], jnp.where(at < 4 * W, rows[1], rows[2]))

    def lift_rows(parts):
        size = sum(n for _, n in parts)
        patch = jnp.concatenate([gather(g, lo, n) for g in range(NG) for lo, n in parts], axis=0)
        for q in range(G // KB):
            h = jnp.dot(patch, lift_m[:, q * 256 : q * 256 + 256], preferred_element_type=F32)
            h = jnp.maximum(h + lift_bias4, 0.0).astype(BF16)
            for g in range(NG):
                at = g * size
                for lo, n in parts:
                    hid[g * KB + q + 1, lo : lo + n, :] = h[at : at + n]
                    at += n

    def mix_rows(parts):
        rows = []
        for kb in range(1, NB + 1):
            for lo, n in parts:
                at = [pl.ds(lo + b * C, n) for b in range(3)]
                main = [hid[kb, i, :] for i in at]
                edge = [jnp.where(lane[:n] < O, hid[kb + 1, i, :128], hid[kb - 1, i, 128:]) for i in at]
                rows.append(jnp.concatenate(main + edge, axis=1))
        total = jnp.dot(jnp.concatenate(rows, axis=0), mix_m[...], preferred_element_type=F32)
        total = jnp.maximum(total + mix_bias4, 0.0).astype(BF16)
        at = 0
        for kb in range(NB):
            for lo, n in parts:
                mixed[kb, lo : lo + n, :] = total[at : at + n]
                at += n

    lift_rows([(2 * C, 6 * C)])
    mix_rows([(2 * C, 4 * C)])

    @pl.when(has_above)
    def _():
        down.wait_recv()

    @pl.when(has_below)
    def _():
        up.wait_recv()

    outer = jnp.dot(
        halo[...].reshape(4 * C, 256), fwd_v[...], preferred_element_type=F32
    ).astype(BF16)
    for g in range(NG):
        spec[g, : 2 * C, :] = outer[: 2 * C, g * 128 : g * 128 + 128]
        spec[g, 10 * C :, :] = outer[2 * C :, g * 128 : g * 128 + 128]
    lift_rows([(0, 2 * C), (8 * C, 2 * C)])

    top = jnp.full((C, 256), jnp.where(has_above, 1.0, 0.0), F32).astype(BF16)
    bottom = jnp.full((C, 256), jnp.where(has_below, 1.0, 0.0), F32).astype(BF16)
    for kb in range(1, NB + 1):
        hid[kb, :C, :] = hid[kb, :C, :] * top
        hid[kb, 9 * C :, :] = hid[kb, 9 * C :, :] * bottom
    mix_rows([(0, 2 * C), (6 * C, 2 * C)])
    u = lax.dot_general(
        proj4,
        mixed[...].reshape(NB * 8 * C, 256),
        (((1,), (1,)), ((), ())),
        preferred_element_type=F32,
    )
    update = jnp.concatenate(
        [u[:, kb * 128 : kb * 128 + 128] + proj_bias4 for kb in range(NB)], axis=0
    ).astype(BF16)
    back = jnp.dot(inv_v[...], update, preferred_element_type=F32)
    sent2[...] = back.astype(BF16).reshape(NF, 2 * T, 128)

    second = [
        pltpu.make_async_remote_copy(
            src_ref=sent2.at[p],
            dst_ref=got2.at[f],
            send_sem=send2_sem.at[i],
            recv_sem=recv2_sem.at[i],
            device_id={"frames": p},
            device_id_type=MESH,
        )
        for i, p in enumerate(peers)
    ]
    for c in second:
        c.start()
    got2[f] = sent2[f]
    for c in second:
        c.wait_recv()
    for ri in range(2):
        parts = [got2[i, ri * T : ri * T + T, :].astype(F32) for i in range(NF)]
        for i, part in enumerate(butterfly(parts)):
            at = (ri, pl.ds(i, T, stride=R), slice(None))
            out[at] = part + series_f[at]
    for c in first + second:
        c.wait_send()

    @pl.when(has_below)
    def _():
        down.wait_send()

    @pl.when(has_above)
    def _():
        up.wait_send()


def per_device(series, lift_weight, lift_bias, mix_weight, mix_bias, proj_weight, proj_bias):
    n_rows = lax.axis_size("rows")
    args = (
        series,
        jnp.asarray(forward_table()),
        jnp.asarray(inverse_table()),
        jnp.asarray(place_table()),
        lift_weight,
        lift_bias[None],
        mix_weight,
        mix_bias[None],
        proj_weight.T,
        proj_bias[None],
    )
    scratch = [pltpu.VMEM(a.shape, a.dtype) for a in args]
    out = pl.pallas_call(
        functools.partial(kernel, n_rows),
        out_shape=pltpu.VMEM((2, T * R, 128), F32),
        in_specs=[pl.BlockSpec(memory_space=pltpu.HBM)] * len(args),
        out_specs=pl.BlockSpec(memory_space=pltpu.VMEM),
        scratch_shapes=scratch
        + [
            pltpu.VMEM((2, T * R, 128), F32),
            pltpu.VMEM((NF, 2 * T, 128), BF16),
            pltpu.VMEM((NF, 2 * T, 128), BF16),
            pltpu.VMEM((R * C, 256), BF16),
            pltpu.VMEM((2, 2 * C, 256), BF16),
            pltpu.VMEM((NG, 12 * C, 128), BF16),
            pltpu.VMEM((32, 128), F32),
            pltpu.VMEM((8, O), F32),
            pltpu.VMEM((128, G * O), BF16),
            pltpu.VMEM((1152, 256), BF16),
            pltpu.VMEM((NB + 2, 10 * C, 256), BF16),
            pltpu.VMEM((NB, R * C, 256), BF16),
            pltpu.VMEM((NF, 2 * T, 128), BF16),
            pltpu.VMEM((NF, 2 * T, 128), BF16),
            pltpu.SemaphoreType.DMA((len(args),)),
            pltpu.SemaphoreType.DMA((NF - 1,)),
            pltpu.SemaphoreType.DMA((NF - 1,)),
            pltpu.SemaphoreType.DMA((2,)),
            pltpu.SemaphoreType.DMA((2,)),
            pltpu.SemaphoreType.DMA((NF - 1,)),
            pltpu.SemaphoreType.DMA((NF - 1,)),
        ],
        compiler_params=pltpu.CompilerParams(
            collective_id=0, has_side_effects=True, vmem_limit_bytes=56 * 1024 * 1024
        ),
    )(*args)
    return jnp.concatenate((out[0], out[1]), axis=1).reshape(T, 1, R, 256)


def solution(mesh):
    return jax.shard_map(
        per_device,
        mesh=mesh,
        in_specs=(P("frames", None, "rows", None), P(), P(), P(), P(), P(), P()),
        out_specs=P("frames", None, "rows", None),
        check_vma=False,
    )
```

```python
import functools
import math

import jax
import jax.numpy as jnp
import ml_dtypes
import numpy as np
from jax import lax
from jax.experimental import pallas as pl
from jax.experimental.pallas import tpu as pltpu
from jax.sharding import PartitionSpec as P

MESH = pl.DeviceIdType.MESH
BF16 = jnp.bfloat16
F32 = jnp.float32

NF = 8
T = 16
N = 128
R = 8
C = 16
O = 64
KB = 4
NB = N // KB
G = 16
NG = N // G
W = G + 2


def forward_table():
    k = np.arange(N)
    t = np.arange(N)
    angle = (2.0 * math.pi / N * (((k[:, None] - N // 2) * t[None, :]) % N)).astype(np.float32)
    scale = np.float32(1.0 / math.sqrt(N))
    re = (np.cos(angle) * scale).astype(ml_dtypes.bfloat16).astype(np.float32)
    im = (-np.sin(angle) * scale).astype(ml_dtypes.bfloat16).astype(np.float32)
    full = np.zeros((NF, 2, T, NG, 128), np.float32)
    for g in range(NG):
        for w in range(W):
            kk = g * G + w - 1
            if not 0 <= kk < N:
                continue
            a = re[kk].reshape(NF, T)
            b = im[kk].reshape(NF, T)
            for tap in range(3):
                lane = tap * 2 * W + w * 2
                full[:, 0, :, g, lane] = a
                full[:, 1, :, g, lane] = -b
                full[:, 0, :, g, lane + 1] = b
                full[:, 1, :, g, lane + 1] = a
    return full.transpose(1, 0, 2, 3, 4).reshape(2 * NF * T, NG * 128).astype(ml_dtypes.bfloat16)


def inverse_table():
    k = np.arange(N)
    t = np.arange(N)
    angle = (2.0 * math.pi / N * (((k[:, None] - N // 2) * t[None, :]) % N)).astype(np.float32).T
    scale = np.float32(1.0 / math.sqrt(N))
    re = (np.cos(angle) * scale).reshape(NF, T, N)
    im = (np.sin(angle) * scale).reshape(NF, T, N)
    full = np.zeros((NF, 2, T, N, 2), np.float32)
    full[:, 0, :, :, 0] = re
    full[:, 0, :, :, 1] = -im
    full[:, 1, :, :, 0] = im
    full[:, 1, :, :, 1] = re
    return full.reshape(NF * 2 * T, N * 2).astype(ml_dtypes.bfloat16)


def place_table():
    full = np.zeros((G // KB, 128, KB, 32), np.float32)
    for q in range(G // KB):
        for j in range(KB):
            for a in range(3):
                for b in range(3):
                    for i in range(2):
                        full[q, b * 2 * W + (q * KB + j + a) * 2 + i, j, (a * 3 + b) * 2 + i] = 1
    return full.reshape(G // KB, 128, 128).astype(ml_dtypes.bfloat16)


PARTNERS = (5, 7, 3, 1, 4, 6, 2)


def partner(f, m):
    for bit in range(3):
        if m >> bit & 1:
            f = f + (1 << bit) * (1 - 2 * (f // (1 << bit) % 2))
    return f


def butterfly(parts):
    lane = lax.broadcasted_iota(jnp.int32, parts[0].shape, 1)
    for bit in range(3):
        step = 1 << bit
        upper = ((lane >> (4 + bit)) & 1) == 1
        out = list(parts)
        for i in range(8):
            if i & step:
                continue
            lo, hi = parts[i], parts[i + step]
            out[i] = jnp.where(upper, pltpu.roll(hi, 16 * step, 1), lo)
            out[i + step] = jnp.where(upper, hi, pltpu.roll(lo, 128 - 16 * step, 1))
        parts = out
    return parts


def kernel(
    n_rows,
    series,
    fwd,
    inv,
    place,
    lift,
    lift_bias,
    mix,
    mix_bias,
    proj,
    proj_bias,
    out,
    series_v,
    fwd_v,
    inv_v,
    place_v,
    lift_v,
    lift_bias_v,
    mix_v,
    mix_bias_v,
    proj_v,
    proj_bias_v,
    series_f,
    sent,
    edge,
    got,
    halo,
    xt,
    spec,
    taps,
    ends,
    lift_m,
    mix_m,
    hid,
    mixed,
    sent2,
    got2,
    load_sem,
    send_sem,
    recv_sem,
    halo_send_sem,
    halo_recv_sem,
    send2_sem,
    recv2_sem,
):
    f = lax.axis_index("frames")
    r = lax.axis_index("rows")
    above = lax.rem(r + n_rows - 1, n_rows)
    below = lax.rem(r + 1, n_rows)
    has_above = r > 0
    has_below = r < n_rows - 1
    peers = [partner(f, m) for m in PARTNERS]

    barrier = pltpu.get_barrier_semaphore()
    for p in peers:
        pl.semaphore_signal(barrier, inc=1, device_id={"frames": p}, device_id_type=MESH)

    for has, near in ((has_above, above), (has_below, below)):

        @pl.when(has)
        def _():
            for p in peers + [f]:
                pl.semaphore_signal(
                    barrier, inc=1, device_id={"frames": p, "rows": near}, device_id_type=MESH
                )

    loads = [
        pltpu.make_async_copy(a, b, load_sem.at[i])
        for i, (a, b) in enumerate(
            (
                (series, series_v),
                (mix, mix_v),
                (lift, lift_v),
                (place, place_v),
                (fwd, fwd_v),
                (inv, inv_v),
                (lift_bias, lift_bias_v),
                (mix_bias, mix_bias_v),
                (proj, proj_v),
                (proj_bias, proj_bias_v),
            )
        )
    ]
    for c in loads:
        c.start()

    loads[0].wait()
    for ri in range(2):
        series_f[ri] = series_v[:, 0, :, ri * 128 : ri * 128 + 128].astype(F32).reshape(T * R, 128)
    tiles = [
        butterfly([series_f[ri, pl.ds(i, T, stride=R), :] for i in range(R)]) for ri in range(2)
    ]
    quarter = lax.broadcasted_iota(jnp.int32, (T, 128), 1) // (2 * C)
    for i, (re, im) in enumerate(zip(*tiles)):
        sent[i, :T, :] = re.astype(BF16)
        sent[i, T:, :] = im.astype(BF16)
        low = jnp.where(quarter == 0, re, pltpu.roll(im, 2 * C, 1))
        high = jnp.where(quarter == 2, pltpu.roll(re, 128 - 2 * C, 1), im)
        edge[i] = jnp.where(quarter < 2, low, high).astype(BF16)

    neighbours = jnp.where(has_above, 1, 0) + jnp.where(has_below, 1, 0)
    pl.semaphore_wait(barrier, NF - 1 + NF * neighbours)
    own = [
        pltpu.make_async_remote_copy(
            src_ref=sent.at[p],
            dst_ref=got.at[f],
            send_sem=send_sem.at[i],
            recv_sem=recv_sem.at[i],
            device_id={"frames": p},
            device_id_type=MESH,
        )
        for i, p in enumerate(peers)
    ]
    down, up = (
        [
            pltpu.make_async_remote_copy(
                src_ref=edge.at[p],
                dst_ref=halo.at[side, f],
                send_sem=halo_send_sem.at[side, i],
                recv_sem=halo_recv_sem.at[side, i],
                device_id={"frames": p, "rows": near},
                device_id_type=MESH,
            )
            for i, p in enumerate(peers + [f])
        ]
        for side, near in ((0, below), (1, above))
    )

    for c in own:
        c.start()

    @pl.when(has_below)
    def _():
        for c in down:
            c.start()

    @pl.when(has_above)
    def _():
        for c in up:
            c.start()

    got[f] = sent[f]

    @pl.when(r == 0)
    def _():
        halo[0] = jnp.zeros(halo.shape[1:], BF16)

    @pl.when(r == n_rows - 1)
    def _():
        halo[1] = jnp.zeros(halo.shape[1:], BF16)

    for c in loads[1:]:
        c.wait()
    taps[...] = jnp.zeros(taps.shape, F32)
    for a in range(3):
        for b in range(3):
            taps[(a * 3 + b) * 2 : (a * 3 + b) * 2 + 2, :O] = lift_v[a, b].astype(F32)
    left = taps[...]
    right = pltpu.roll(left, O, 1)
    none = jnp.zeros_like(left)
    lift4 = jnp.concatenate(
        [jnp.concatenate(p, axis=1) for p in ((left, none), (right, none), (none, left), (none, right))],
        axis=0,
    ).astype(BF16)
    for q in range(G // KB):
        lift_m[:, q * 256 : q * 256 + 256] = jnp.dot(
            place_v[q], lift4, preferred_element_type=F32
        ).astype(BF16)
    for k in range(KB):
        ends[k * 2 : k * 2 + 2, :] = proj_v[...].astype(F32)
    proj4 = jnp.concatenate([ends[...]] * KB, axis=1)
    proj4 = jnp.where(
        lax.broadcasted_iota(jnp.int32, proj4.shape, 0) // 2
        == lax.broadcasted_iota(jnp.int32, proj4.shape, 1) // O,
        proj4,
        0.0,
    ).astype(BF16)
    lift_bias4 = jnp.concatenate([lift_bias_v[...]] * KB, axis=1)
    mix_bias4 = jnp.concatenate([mix_bias_v[...]] * KB, axis=1)
    proj_bias4 = jnp.where(
        lax.broadcasted_iota(jnp.int32, (8, 128), 0) % 2 == 0,
        jnp.broadcast_to(proj_bias_v[:, :1], (8, 128)),
        jnp.broadcast_to(proj_bias_v[:, 1:], (8, 128)),
    )
    zero = jnp.zeros((O, O), BF16)
    for b in range(3):
        t0, t1, t2 = (mix_v[a, b] for a in range(3))
        rows = (
            (t1, t0, zero, zero),
            (t2, t1, t0, zero),
            (zero, t2, t1, t0),
            (zero, zero, t2, t1),
        )
        for j, row in enumerate(rows):
            mix_m[b * 256 + j * O : b * 256 + j * O + O, :] = jnp.concatenate(row, axis=1)
        mix_m[768 + b * 128 : 768 + b * 128 + O, :] = jnp.concatenate((zero, zero, zero, t2), axis=1)
        mix_m[768 + b * 128 + O : 768 + b * 128 + 128, :] = jnp.concatenate((t0, zero, zero, zero), axis=1)
    hid[0] = jnp.zeros(hid.shape[1:], BF16)
    hid[NB + 1] = jnp.zeros(hid.shape[1:], BF16)

    for c in own:
        c.wait_recv()

    @pl.when(has_above)
    def _():
        for c in down:
            c.wait_recv()

    @pl.when(has_below)
    def _():
        for c in up:
            c.wait_recv()

    quarter = lax.broadcasted_iota(jnp.int32, (NF * T, 128), 1) // (2 * C)
    near = jnp.where(quarter < 2, halo[1].reshape(NF * T, 128), halo[0].reshape(NF * T, 128)).T
    for ri in range(2):
        at = slice(ri * 128, ri * 128 + 128)
        xt[: 2 * C, at] = near[(2 + ri) * 2 * C : (3 + ri) * 2 * C]
        xt[2 * C : 10 * C, at] = got[:, ri * T : ri * T + T, :].reshape(NF * T, 128).T
        xt[10 * C :, at] = near[ri * 2 * C : (1 + ri) * 2 * C]
    spectrum = jnp.dot(xt[...], fwd_v[...], preferred_element_type=F32).astype(BF16)
    for g in range(NG):
        spec[g] = spectrum[:, g * 128 : g * 128 + 128]

    lane = lax.broadcasted_iota(jnp.int32, (10 * C, 128), 1)

    def gather(g, lo, size):
        rows = [spec[g, lo + b * C : lo + b * C + size, :] for b in range(3)]
        at = lane[:size]
        return jnp.where(at < 2 * W, rows[0], jnp.where(at < 4 * W, rows[1], rows[2]))

    def lift_rows(parts):
        size = sum(n for _, n in parts)
        patch = jnp.concatenate([gather(g, lo, n) for g in range(NG) for lo, n in parts], axis=0)
        for q in range(G // KB):
            h = jnp.dot(patch, lift_m[:, q * 256 : q * 256 + 256], preferred_element_type=F32)
            h = jnp.maximum(h + lift_bias4, 0.0).astype(BF16)
            for g in range(NG):
                at = g * size
                for lo, n in parts:
                    hid[g * KB + q + 1, lo : lo + n, :] = h[at : at + n]
                    at += n

    def mix_rows(parts):
        rows = []
        for kb in range(1, NB + 1):
            for lo, n in parts:
                at = [pl.ds(lo + b * C, n) for b in range(3)]
                main = [hid[kb, i, :] for i in at]
                side = [jnp.where(lane[:n] < O, hid[kb + 1, i, :128], hid[kb - 1, i, 128:]) for i in at]
                rows.append(jnp.concatenate(main + side, axis=1))
        total = jnp.dot(jnp.concatenate(rows, axis=0), mix_m[...], preferred_element_type=F32)
        total = jnp.maximum(total + mix_bias4, 0.0).astype(BF16)
        at = 0
        for kb in range(NB):
            for lo, n in parts:
                mixed[kb, lo : lo + n, :] = total[at : at + n]
                at += n

    lift_rows([(0, 10 * C)])
    top = jnp.full((C, 256), jnp.where(has_above, 1.0, 0.0), F32).astype(BF16)
    bottom = jnp.full((C, 256), jnp.where(has_below, 1.0, 0.0), F32).astype(BF16)
    for kb in range(1, NB + 1):
        hid[kb, :C, :] = hid[kb, :C, :] * top
        hid[kb, 9 * C :, :] = hid[kb, 9 * C :, :] * bottom
    mix_rows([(0, 8 * C)])
    u = lax.dot_general(
        proj4,
        mixed[...].reshape(NB * 8 * C, 256),
        (((1,), (1,)), ((), ())),
        preferred_element_type=F32,
    )
    update = jnp.concatenate(
        [u[:, kb * 128 : kb * 128 + 128] + proj_bias4 for kb in range(NB)], axis=0
    ).astype(BF16)
    back = jnp.dot(inv_v[...], update, preferred_element_type=F32)
    sent2[...] = back.astype(BF16).reshape(NF, 2 * T, 128)

    second = [
        pltpu.make_async_remote_copy(
            src_ref=sent2.at[p],
            dst_ref=got2.at[f],
            send_sem=send2_sem.at[i],
            recv_sem=recv2_sem.at[i],
            device_id={"frames": p},
            device_id_type=MESH,
        )
        for i, p in enumerate(peers)
    ]
    for c in second:
        c.start()
    got2[f] = sent2[f]
    for c in second:
        c.wait_recv()
    for ri in range(2):
        parts = [got2[i, ri * T : ri * T + T, :].astype(F32) for i in range(NF)]
        for i, part in enumerate(butterfly(parts)):
            at = (ri, pl.ds(i, T, stride=R), slice(None))
            out[at] = part + series_f[at]
    for c in own + second:
        c.wait_send()

    @pl.when(has_below)
    def _():
        for c in down:
            c.wait_send()

    @pl.when(has_above)
    def _():
        for c in up:
            c.wait_send()


def per_device(series, lift_weight, lift_bias, mix_weight, mix_bias, proj_weight, proj_bias):
    n_rows = lax.axis_size("rows")
    args = (
        series,
        jnp.asarray(forward_table()),
        jnp.asarray(inverse_table()),
        jnp.asarray(place_table()),
        lift_weight,
        lift_bias[None],
        mix_weight,
        mix_bias[None],
        proj_weight.T,
        proj_bias[None],
    )
    scratch = [pltpu.VMEM(a.shape, a.dtype) for a in args]
    out = pl.pallas_call(
        functools.partial(kernel, n_rows),
        out_shape=pltpu.VMEM((2, T * R, 128), F32),
        in_specs=[pl.BlockSpec(memory_space=pltpu.HBM)] * len(args),
        out_specs=pl.BlockSpec(memory_space=pltpu.VMEM),
        scratch_shapes=scratch
        + [
            pltpu.VMEM((2, T * R, 128), F32),
            pltpu.VMEM((NF, 2 * T, 128), BF16),
            pltpu.VMEM((NF, T, 128), BF16),
            pltpu.VMEM((NF, 2 * T, 128), BF16),
            pltpu.VMEM((2, NF, T, 128), BF16),
            pltpu.VMEM((12 * C, 256), BF16),
            pltpu.VMEM((NG, 12 * C, 128), BF16),
            pltpu.VMEM((32, 128), F32),
            pltpu.VMEM((8, O), F32),
            pltpu.VMEM((128, G * O), BF16),
            pltpu.VMEM((1152, 256), BF16),
            pltpu.VMEM((NB + 2, 10 * C, 256), BF16),
            pltpu.VMEM((NB, R * C, 256), BF16),
            pltpu.VMEM((NF, 2 * T, 128), BF16),
            pltpu.VMEM((NF, 2 * T, 128), BF16),
            pltpu.SemaphoreType.DMA((len(args),)),
            pltpu.SemaphoreType.DMA((NF - 1,)),
            pltpu.SemaphoreType.DMA((NF - 1,)),
            pltpu.SemaphoreType.DMA((2, NF)),
            pltpu.SemaphoreType.DMA((2, NF)),
            pltpu.SemaphoreType.DMA((NF - 1,)),
            pltpu.SemaphoreType.DMA((NF - 1,)),
        ],
        compiler_params=pltpu.CompilerParams(
            collective_id=0, has_side_effects=True, vmem_limit_bytes=56 * 1024 * 1024
        ),
    )(*args)
    return jnp.concatenate((out[0], out[1]), axis=1).reshape(T, 1, R, 256)


def solution(mesh):
    return jax.shard_map(
        per_device,
        mesh=mesh,
        in_specs=(P("frames", None, "rows", None), P(), P(), P(), P(), P(), P()),
        out_specs=P("frames", None, "rows", None),
        check_vma=False,
    )
```

```python
import functools
import math

import jax
import jax.numpy as jnp
import ml_dtypes
import numpy as np
from jax import lax
from jax.experimental import pallas as pl
from jax.experimental.pallas import tpu as pltpu
from jax.sharding import PartitionSpec as P

MESH = pl.DeviceIdType.MESH
BF16 = jnp.bfloat16
F32 = jnp.float32

NF = 8
T = 16
N = 128
R = 8
C = 16
O = 64
KB = 4
G = 16
NG = N // G
W = G + 2


def forward_table():
    k = np.arange(N)
    t = np.arange(N)
    angle = (2.0 * math.pi / N * (((k[:, None] - N // 2) * t[None, :]) % N)).astype(np.float32)
    scale = np.float32(1.0 / math.sqrt(N))
    re = (np.cos(angle) * scale).astype(ml_dtypes.bfloat16).astype(np.float32)
    im = (-np.sin(angle) * scale).astype(ml_dtypes.bfloat16).astype(np.float32)
    full = np.zeros((NF, 2, T, NG, 128), np.float32)
    for g in range(NG):
        for w in range(W):
            kk = g * G + w - 1
            if not 0 <= kk < N:
                continue
            a = re[kk].reshape(NF, T)
            b = im[kk].reshape(NF, T)
            for tap in range(3):
                lane = tap * 2 * W + w * 2
                full[:, 0, :, g, lane] = a
                full[:, 1, :, g, lane] = -b
                full[:, 0, :, g, lane + 1] = b
                full[:, 1, :, g, lane + 1] = a
    return full.transpose(1, 0, 2, 3, 4).reshape(2 * NF * T, NG * 128).astype(ml_dtypes.bfloat16)


def inverse_table():
    k = np.arange(N)
    t = np.arange(N)
    angle = (2.0 * math.pi / N * (((k[:, None] - N // 2) * t[None, :]) % N)).astype(np.float32).T
    scale = np.float32(1.0 / math.sqrt(N))
    re = (np.cos(angle) * scale).reshape(NF, T, N)
    im = (np.sin(angle) * scale).reshape(NF, T, N)
    full = np.zeros((NF, 2, T, N, 2), np.float32)
    full[:, 0, :, :, 0] = re
    full[:, 0, :, :, 1] = -im
    full[:, 1, :, :, 0] = im
    full[:, 1, :, :, 1] = re
    return full.reshape(NF * 2 * T, N * 2).astype(ml_dtypes.bfloat16)


def place_table():
    full = np.zeros((G // KB, 128, KB, 32), np.float32)
    for q in range(G // KB):
        for j in range(KB):
            for a in range(3):
                for b in range(3):
                    for i in range(2):
                        full[q, b * 2 * W + (q * KB + j + a) * 2 + i, j, (a * 3 + b) * 2 + i] = 1
    return full.reshape(G // KB, 128, 128).astype(ml_dtypes.bfloat16)


PARTNERS = (5, 7, 3, 1, 4, 6, 2)


def partner(f, m):
    for bit in range(3):
        if m >> bit & 1:
            f = f + (1 << bit) * (1 - 2 * (f // (1 << bit) % 2))
    return f


def butterfly(parts):
    lane = lax.broadcasted_iota(jnp.int32, parts[0].shape, 1)
    for bit in range(3):
        step = 1 << bit
        upper = ((lane >> (4 + bit)) & 1) == 1
        out = list(parts)
        for i in range(8):
            if i & step:
                continue
            lo, hi = parts[i], parts[i + step]
            out[i] = jnp.where(upper, pltpu.roll(hi, 16 * step, 1), lo)
            out[i + step] = jnp.where(upper, hi, pltpu.roll(lo, 128 - 16 * step, 1))
        parts = out
    return parts


def kernel(
    n_rows,
    series,
    fwd,
    inv,
    place,
    lift,
    lift_bias,
    mix,
    mix_bias,
    proj,
    proj_bias,
    out,
    series_v,
    fwd_v,
    inv_v,
    place_v,
    lift_v,
    lift_bias_v,
    mix_v,
    mix_bias_v,
    proj_v,
    proj_bias_v,
    series_f,
    sent,
    edge,
    got,
    halo,
    xt,
    spec,
    taps,
    ends,
    lift_m,
    mix_m,
    hid,
    sent2,
    got2,
    load_sem,
    send_sem,
    recv_sem,
    halo_send_sem,
    halo_recv_sem,
    send2_sem,
    recv2_sem,
):
    f = lax.axis_index("frames")
    r = lax.axis_index("rows")
    above = lax.rem(r + n_rows - 1, n_rows)
    below = lax.rem(r + 1, n_rows)
    has_above = r > 0
    has_below = r < n_rows - 1
    peers = [partner(f, m) for m in PARTNERS]

    barrier = pltpu.get_barrier_semaphore()
    for p in peers:
        pl.semaphore_signal(barrier, inc=1, device_id={"frames": p}, device_id_type=MESH)

    for has, near in ((has_above, above), (has_below, below)):

        @pl.when(has)
        def _():
            for p in peers + [f]:
                pl.semaphore_signal(
                    barrier, inc=1, device_id={"frames": p, "rows": near}, device_id_type=MESH
                )

    loads = [
        pltpu.make_async_copy(a, b, load_sem.at[i])
        for i, (a, b) in enumerate(
            (
                (series, series_v),
                (mix, mix_v),
                (lift, lift_v),
                (place, place_v),
                (fwd, fwd_v),
                (inv, inv_v),
                (lift_bias, lift_bias_v),
                (mix_bias, mix_bias_v),
                (proj, proj_v),
                (proj_bias, proj_bias_v),
            )
        )
    ]
    for c in loads:
        c.start()

    loads[0].wait()
    for ri in range(2):
        series_f[ri] = series_v[:, 0, :, ri * 128 : ri * 128 + 128].astype(F32).reshape(T * R, 128)
    tiles = [
        butterfly([series_f[ri, pl.ds(i, T, stride=R), :] for i in range(R)]) for ri in range(2)
    ]
    quarter = lax.broadcasted_iota(jnp.int32, (T, 128), 1) // (2 * C)
    for i, (re, im) in enumerate(zip(*tiles)):
        sent[i, :T, :] = re.astype(BF16)
        sent[i, T:, :] = im.astype(BF16)
        low = jnp.where(quarter == 0, re, pltpu.roll(im, 2 * C, 1))
        high = jnp.where(quarter == 2, pltpu.roll(re, 128 - 2 * C, 1), im)
        edge[i] = jnp.where(quarter < 2, low, high).astype(BF16)

    neighbours = jnp.where(has_above, 1, 0) + jnp.where(has_below, 1, 0)
    pl.semaphore_wait(barrier, NF - 1 + NF * neighbours)
    own = [
        pltpu.make_async_remote_copy(
            src_ref=sent.at[p],
            dst_ref=got.at[f],
            send_sem=send_sem.at[i],
            recv_sem=recv_sem.at[i],
            device_id={"frames": p},
            device_id_type=MESH,
        )
        for i, p in enumerate(peers)
    ]
    down, up = (
        [
            pltpu.make_async_remote_copy(
                src_ref=edge.at[p],
                dst_ref=halo.at[side, f],
                send_sem=halo_send_sem.at[side, i],
                recv_sem=halo_recv_sem.at[side, i],
                device_id={"frames": p, "rows": near},
                device_id_type=MESH,
            )
            for i, p in enumerate(peers + [f])
        ]
        for side, near in ((0, below), (1, above))
    )

    for c in own:
        c.start()

    @pl.when(has_below)
    def _():
        for c in down:
            c.start()

    @pl.when(has_above)
    def _():
        for c in up:
            c.start()

    got[f] = sent[f]

    @pl.when(r == 0)
    def _():
        halo[0] = jnp.zeros(halo.shape[1:], BF16)

    @pl.when(r == n_rows - 1)
    def _():
        halo[1] = jnp.zeros(halo.shape[1:], BF16)

    for c in loads[1:]:
        c.wait()
    taps[...] = jnp.zeros(taps.shape, F32)
    for a in range(3):
        for b in range(3):
            taps[(a * 3 + b) * 2 : (a * 3 + b) * 2 + 2, :O] = lift_v[a, b].astype(F32)
    left = taps[...]
    right = pltpu.roll(left, O, 1)
    none = jnp.zeros_like(left)
    lift4 = jnp.concatenate(
        [jnp.concatenate(p, axis=1) for p in ((left, none), (right, none), (none, left), (none, right))],
        axis=0,
    ).astype(BF16)
    for q in range(G // KB):
        lift_m[:, q * 256 : q * 256 + 256] = jnp.dot(
            place_v[q], lift4, preferred_element_type=F32
        ).astype(BF16)
    for k in range(KB):
        ends[k * 2 : k * 2 + 2, :] = proj_v[...].astype(F32)
    proj4 = jnp.concatenate([ends[...]] * KB, axis=1)
    pair = lax.broadcasted_iota(jnp.int32, proj4.shape, 1) // O
    proj4 = jnp.where(
        lax.broadcasted_iota(jnp.int32, proj4.shape, 0) // 2 == pair % 2 * 2 + pair // 2, proj4, 0.0
    ).astype(BF16)
    lift_bias4 = jnp.concatenate([lift_bias_v[...]] * KB, axis=1)
    mix_bias4 = jnp.concatenate([mix_bias_v[...]] * KB, axis=1)
    proj_bias4 = jnp.where(
        lax.broadcasted_iota(jnp.int32, (8, 128), 0) % 2 == 0,
        jnp.broadcast_to(proj_bias_v[:, :1], (8, 128)),
        jnp.broadcast_to(proj_bias_v[:, 1:], (8, 128)),
    )
    zero = jnp.zeros((O, O), BF16)
    for w in range(4):

        def taps_of(a):
            return tuple(mix_v[a, w - r2] if 0 <= w - r2 <= 2 else zero for r2 in range(2))

        blank = (zero, zero)
        rows = (
            taps_of(1) + taps_of(0),
            taps_of(2) + taps_of(1),
            blank + taps_of(2),
            taps_of(0) + blank,
        )
        for j, row in enumerate(rows):
            at = w * 256 + j * O
            mix_m[at : at + O, :] = jnp.concatenate(row, axis=1)
    hid[0] = jnp.zeros(hid.shape[1:], BF16)
    hid[N // 2 + 1] = jnp.zeros(hid.shape[1:], BF16)

    for c in own:
        c.wait_recv()

    @pl.when(has_above)
    def _():
        for c in down:
            c.wait_recv()

    @pl.when(has_below)
    def _():
        for c in up:
            c.wait_recv()

    quarter = lax.broadcasted_iota(jnp.int32, (NF * T, 128), 1) // (2 * C)
    near = jnp.where(quarter < 2, halo[1].reshape(NF * T, 128), halo[0].reshape(NF * T, 128)).T
    for ri in range(2):
        at = slice(ri * 128, ri * 128 + 128)
        xt[: 2 * C, at] = near[(2 + ri) * 2 * C : (3 + ri) * 2 * C]
        xt[2 * C : 10 * C, at] = got[:, ri * T : ri * T + T, :].reshape(NF * T, 128).T
        xt[10 * C :, at] = near[ri * 2 * C : (1 + ri) * 2 * C]
    spectrum = jnp.dot(xt[...], fwd_v[...], preferred_element_type=F32).astype(BF16)
    for g in range(NG):
        spec[g] = spectrum[:, g * 128 : g * 128 + 128]

    lane = lax.broadcasted_iota(jnp.int32, (10 * C, 128), 1)

    patch = []
    for g in range(NG):
        rows = [spec[g, b * C : b * C + 10 * C, :] for b in range(3)]
        patch.append(jnp.where(lane < 2 * W, rows[0], jnp.where(lane < 4 * W, rows[1], rows[2])))
    patch = jnp.concatenate(patch, axis=0)
    top = jnp.full((C, 128), jnp.where(has_above, 1.0, 0.0), F32).astype(BF16)
    bottom = jnp.full((C, 128), jnp.where(has_below, 1.0, 0.0), F32).astype(BF16)
    for q in range(G // KB):
        h = jnp.dot(patch, lift_m[:, q * 256 : q * 256 + 256], preferred_element_type=F32)
        h = jnp.maximum(h + lift_bias4, 0.0).astype(BF16)
        for g in range(NG):
            at = g * 10 * C
            for half in range(2):
                kp = (g * KB + q) * 2 + half + 1
                cols = slice(half * 128, half * 128 + 128)
                hid[kp, :C, :] = h[at : at + C, cols] * top
                hid[kp, C : 9 * C, :] = h[at + C : at + 9 * C, cols]
                hid[kp, 9 * C :, :] = h[at + 9 * C : at + 10 * C, cols] * bottom

    blocks = []
    for kp in range(1, N // 2 + 1):
        here = hid[kp]
        beside = jnp.where(lane < O, hid[kp + 1], hid[kp - 1])
        for rp in range(R // 2):
            window = [slice((2 * rp + w) * C, (2 * rp + w + 1) * C) for w in range(4)]
            blocks.append(jnp.concatenate([x[at] for at in window for x in (here, beside)], axis=1))
    mixed = jnp.dot(jnp.concatenate(blocks, axis=0), mix_m[...], preferred_element_type=F32)
    mixed = jnp.maximum(mixed + mix_bias4, 0.0).astype(BF16)
    u = lax.dot_general(
        proj4, mixed, (((1,), (1,)), ((), ())), preferred_element_type=F32
    )
    stay = (lax.broadcasted_iota(jnp.int32, (8, 128), 0) < 4) == (
        lax.broadcasted_iota(jnp.int32, (8, 128), 1) < 64
    )
    update = []
    for i in range(N // 4):
        v = u[:, i * 128 : i * 128 + 128]
        v = jnp.where(stay, v, pltpu.roll(pltpu.roll(v, 4, 0), 64, 1))
        update.append(v + proj_bias4)
    update = jnp.concatenate(update, axis=0).astype(BF16)
    back = jnp.dot(inv_v[...], update, preferred_element_type=F32)
    sent2[...] = back.astype(BF16).reshape(NF, 2 * T, 128)

    second = [
        pltpu.make_async_remote_copy(
            src_ref=sent2.at[p],
            dst_ref=got2.at[f],
            send_sem=send2_sem.at[i],
            recv_sem=recv2_sem.at[i],
            device_id={"frames": p},
            device_id_type=MESH,
        )
        for i, p in enumerate(peers)
    ]
    for c in second:
        c.start()
    got2[f] = sent2[f]
    for c in second:
        c.wait_recv()
    for ri in range(2):
        parts = [got2[i, ri * T : ri * T + T, :].astype(F32) for i in range(NF)]
        for i, part in enumerate(butterfly(parts)):
            row = i % 4 * 2 + i // 4
            at = (ri, pl.ds(row, T, stride=R), slice(None))
            out[at] = part + series_f[at]
    for c in own + second:
        c.wait_send()

    @pl.when(has_below)
    def _():
        for c in down:
            c.wait_send()

    @pl.when(has_above)
    def _():
        for c in up:
            c.wait_send()


def per_device(series, lift_weight, lift_bias, mix_weight, mix_bias, proj_weight, proj_bias):
    n_rows = lax.axis_size("rows")
    args = (
        series,
        jnp.asarray(forward_table()),
        jnp.asarray(inverse_table()),
        jnp.asarray(place_table()),
        lift_weight,
        lift_bias[None],
        mix_weight,
        mix_bias[None],
        proj_weight.T,
        proj_bias[None],
    )
    scratch = [pltpu.VMEM(a.shape, a.dtype) for a in args]
    out = pl.pallas_call(
        functools.partial(kernel, n_rows),
        out_shape=pltpu.VMEM((2, T * R, 128), F32),
        in_specs=[pl.BlockSpec(memory_space=pltpu.HBM)] * len(args),
        out_specs=pl.BlockSpec(memory_space=pltpu.VMEM),
        scratch_shapes=scratch
        + [
            pltpu.VMEM((2, T * R, 128), F32),
            pltpu.VMEM((NF, 2 * T, 128), BF16),
            pltpu.VMEM((NF, T, 128), BF16),
            pltpu.VMEM((NF, 2 * T, 128), BF16),
            pltpu.VMEM((2, NF, T, 128), BF16),
            pltpu.VMEM((12 * C, 256), BF16),
            pltpu.VMEM((NG, 12 * C, 128), BF16),
            pltpu.VMEM((32, 128), F32),
            pltpu.VMEM((8, O), F32),
            pltpu.VMEM((128, G * O), BF16),
            pltpu.VMEM((1024, 256), BF16),
            pltpu.VMEM((N // 2 + 2, 10 * C, 128), BF16),
            pltpu.VMEM((NF, 2 * T, 128), BF16),
            pltpu.VMEM((NF, 2 * T, 128), BF16),
            pltpu.SemaphoreType.DMA((len(args),)),
            pltpu.SemaphoreType.DMA((NF - 1,)),
            pltpu.SemaphoreType.DMA((NF - 1,)),
            pltpu.SemaphoreType.DMA((2, NF)),
            pltpu.SemaphoreType.DMA((2, NF)),
            pltpu.SemaphoreType.DMA((NF - 1,)),
            pltpu.SemaphoreType.DMA((NF - 1,)),
        ],
        compiler_params=pltpu.CompilerParams(
            collective_id=0, has_side_effects=True, vmem_limit_bytes=56 * 1024 * 1024
        ),
    )(*args)
    return jnp.concatenate((out[0], out[1]), axis=1).reshape(T, 1, R, 256)


def solution(mesh):
    return jax.shard_map(
        per_device,
        mesh=mesh,
        in_specs=(P("frames", None, "rows", None), P(), P(), P(), P(), P(), P()),
        out_specs=P("frames", None, "rows", None),
        check_vma=False,
    )
```

```python
import functools
import math

import jax
import jax.numpy as jnp
import ml_dtypes
import numpy as np
from jax import lax
from jax.experimental import pallas as pl
from jax.experimental.pallas import tpu as pltpu
from jax.sharding import PartitionSpec as P

MESH = pl.DeviceIdType.MESH
BF16 = jnp.bfloat16
F32 = jnp.float32

NF = 8
T = 16
N = 128
R = 8
C = 16
O = 64
KB = 4
G = 16
NG = N // G
W = G + 2


def forward_table():
    k = np.arange(N)
    t = np.arange(N)
    angle = (2.0 * math.pi / N * (((k[:, None] - N // 2) * t[None, :]) % N)).astype(np.float32)
    scale = np.float32(1.0 / math.sqrt(N))
    re = (np.cos(angle) * scale).astype(ml_dtypes.bfloat16).astype(np.float32)
    im = (-np.sin(angle) * scale).astype(ml_dtypes.bfloat16).astype(np.float32)
    full = np.zeros((NF, 2, T, NG, 128), np.float32)
    for g in range(NG):
        for w in range(W):
            kk = g * G + w - 1
            if not 0 <= kk < N:
                continue
            a = re[kk].reshape(NF, T)
            b = im[kk].reshape(NF, T)
            for tap in range(3):
                lane = tap * 2 * W + w * 2
                full[:, 0, :, g, lane] = a
                full[:, 1, :, g, lane] = -b
                full[:, 0, :, g, lane + 1] = b
                full[:, 1, :, g, lane + 1] = a
    return full.transpose(1, 0, 2, 3, 4).reshape(2 * NF * T, NG * 128).astype(ml_dtypes.bfloat16)


def inverse_table():
    k = np.arange(N)
    t = np.arange(N)
    angle = (2.0 * math.pi / N * (((k[:, None] - N // 2) * t[None, :]) % N)).astype(np.float32).T
    scale = np.float32(1.0 / math.sqrt(N))
    re = (np.cos(angle) * scale).reshape(NF, T, N)
    im = (np.sin(angle) * scale).reshape(NF, T, N)
    full = np.zeros((NF, 2, T, N, 2), np.float32)
    full[:, 0, :, :, 0] = re
    full[:, 0, :, :, 1] = -im
    full[:, 1, :, :, 0] = im
    full[:, 1, :, :, 1] = re
    return full.reshape(NF * 2 * T, N * 2).astype(ml_dtypes.bfloat16)


def place_table():
    full = np.zeros((G // KB, 128, KB, 32), np.float32)
    for q in range(G // KB):
        for j in range(KB):
            for a in range(3):
                for b in range(3):
                    for i in range(2):
                        full[q, b * 2 * W + (q * KB + j + a) * 2 + i, j, (a * 3 + b) * 2 + i] = 1
    return full.reshape(G // KB, 128, 128).astype(ml_dtypes.bfloat16)


PARTNERS = (5, 7, 3, 1, 4, 6, 2)


def partner(f, m):
    for bit in range(3):
        if m >> bit & 1:
            f = f + (1 << bit) * (1 - 2 * (f // (1 << bit) % 2))
    return f


def butterfly(parts):
    lane = lax.broadcasted_iota(jnp.int32, parts[0].shape, 1)
    for bit in range(3):
        step = 1 << bit
        upper = ((lane >> (4 + bit)) & 1) == 1
        out = list(parts)
        for i in range(8):
            if i & step:
                continue
            lo, hi = parts[i], parts[i + step]
            out[i] = jnp.where(upper, pltpu.roll(hi, 16 * step, 1), lo)
            out[i + step] = jnp.where(upper, hi, pltpu.roll(lo, 128 - 16 * step, 1))
        parts = out
    return parts


def kernel(
    n_rows,
    series,
    fwd,
    inv,
    place,
    lift,
    lift_bias,
    mix,
    mix_bias,
    proj,
    proj_bias,
    out,
    series_v,
    fwd_v,
    inv_v,
    place_v,
    lift_v,
    lift_bias_v,
    mix_v,
    mix_bias_v,
    proj_v,
    proj_bias_v,
    series_f,
    sent,
    edge,
    got,
    halo,
    xt,
    spec,
    taps,
    ends,
    lift_m,
    mix_m,
    hid,
    sent2,
    got2,
    load_sem,
    send_sem,
    recv_sem,
    halo_send_sem,
    halo_recv_sem,
    send2_sem,
    recv2_sem,
):
    f = lax.axis_index("frames")
    r = lax.axis_index("rows")
    above = lax.rem(r + n_rows - 1, n_rows)
    below = lax.rem(r + 1, n_rows)
    has_above = r > 0
    has_below = r < n_rows - 1
    peers = [partner(f, m) for m in PARTNERS]

    loads = [
        pltpu.make_async_copy(a, b, load_sem.at[i])
        for i, (a, b) in enumerate(
            (
                (series, series_v),
                (mix, mix_v),
                (lift, lift_v),
                (place, place_v),
                (fwd, fwd_v),
                (inv, inv_v),
                (lift_bias, lift_bias_v),
                (mix_bias, mix_bias_v),
                (proj, proj_v),
                (proj_bias, proj_bias_v),
            )
        )
    ]
    loads[0].start()

    barrier = pltpu.get_barrier_semaphore()
    for p in peers:
        pl.semaphore_signal(barrier, inc=1, device_id={"frames": p}, device_id_type=MESH)

    for has, near in ((has_above, above), (has_below, below)):

        @pl.when(has)
        def _():
            for p in peers + [f]:
                pl.semaphore_signal(
                    barrier, inc=1, device_id={"frames": p, "rows": near}, device_id_type=MESH
                )

    for c in loads[1:]:
        c.start()

    loads[0].wait()
    for ri in range(2):
        series_f[ri] = series_v[:, 0, :, ri * 128 : ri * 128 + 128].astype(F32).reshape(T * R, 128)
    tiles = [
        butterfly([series_f[ri, pl.ds(i, T, stride=R), :] for i in range(R)]) for ri in range(2)
    ]
    quarter = lax.broadcasted_iota(jnp.int32, (T, 128), 1) // (2 * C)
    for i, (re, im) in enumerate(zip(*tiles)):
        sent[i, :T, :] = re.astype(BF16)
        sent[i, T:, :] = im.astype(BF16)
        low = jnp.where(quarter == 0, re, pltpu.roll(im, 2 * C, 1))
        high = jnp.where(quarter == 2, pltpu.roll(re, 128 - 2 * C, 1), im)
        edge[i] = jnp.where(quarter < 2, low, high).astype(BF16)

    neighbours = jnp.where(has_above, 1, 0) + jnp.where(has_below, 1, 0)
    pl.semaphore_wait(barrier, NF - 1 + NF * neighbours)
    own = [
        pltpu.make_async_remote_copy(
            src_ref=sent.at[p],
            dst_ref=got.at[f],
            send_sem=send_sem.at[i],
            recv_sem=recv_sem.at[i],
            device_id={"frames": p},
            device_id_type=MESH,
        )
        for i, p in enumerate(peers)
    ]
    down, up = (
        [
            pltpu.make_async_remote_copy(
                src_ref=edge.at[p],
                dst_ref=halo.at[side, f],
                send_sem=halo_send_sem.at[side, i],
                recv_sem=halo_recv_sem.at[side, i],
                device_id={"frames": p, "rows": near},
                device_id_type=MESH,
            )
            for i, p in enumerate(peers + [f])
        ]
        for side, near in ((0, below), (1, above))
    )

    for c in own[:3]:
        c.start()

    @pl.when(has_below)
    def _():
        for c in down:
            c.start()

    @pl.when(has_above)
    def _():
        for c in up:
            c.start()

    for c in own[3:]:
        c.start()

    got[f] = sent[f]

    @pl.when(r == 0)
    def _():
        halo[0] = jnp.zeros(halo.shape[1:], BF16)

    @pl.when(r == n_rows - 1)
    def _():
        halo[1] = jnp.zeros(halo.shape[1:], BF16)

    for c in loads[1:]:
        c.wait()
    taps[...] = jnp.zeros(taps.shape, F32)
    for a in range(3):
        for b in range(3):
            taps[(a * 3 + b) * 2 : (a * 3 + b) * 2 + 2, :O] = lift_v[a, b].astype(F32)
    left = taps[...]
    right = pltpu.roll(left, O, 1)
    none = jnp.zeros_like(left)
    lift4 = jnp.concatenate(
        [jnp.concatenate(p, axis=1) for p in ((left, none), (right, none), (none, left), (none, right))],
        axis=0,
    ).astype(BF16)
    for q in range(G // KB):
        lift_m[:, q * 256 : q * 256 + 256] = jnp.dot(
            place_v[q], lift4, preferred_element_type=F32
        ).astype(BF16)
    for k in range(KB):
        ends[k * 2 : k * 2 + 2, :] = proj_v[...].astype(F32)
    proj4 = jnp.concatenate([ends[...]] * KB, axis=1)
    pair = lax.broadcasted_iota(jnp.int32, proj4.shape, 1) // O
    proj4 = jnp.where(
        lax.broadcasted_iota(jnp.int32, proj4.shape, 0) // 2 == pair % 2 * 2 + pair // 2, proj4, 0.0
    ).astype(BF16)
    lift_bias4 = jnp.concatenate([lift_bias_v[...]] * KB, axis=1)
    mix_bias4 = jnp.concatenate([mix_bias_v[...]] * KB, axis=1)
    proj_bias4 = jnp.where(
        lax.broadcasted_iota(jnp.int32, (8, 128), 0) % 2 == 0,
        jnp.broadcast_to(proj_bias_v[:, :1], (8, 128)),
        jnp.broadcast_to(proj_bias_v[:, 1:], (8, 128)),
    )
    zero = jnp.zeros((O, O), BF16)
    for w in range(4):

        def taps_of(a):
            return tuple(mix_v[a, w - r2] if 0 <= w - r2 <= 2 else zero for r2 in range(2))

        blank = (zero, zero)
        rows = (
            taps_of(1) + taps_of(0),
            taps_of(2) + taps_of(1),
            blank + taps_of(2),
            taps_of(0) + blank,
        )
        for j, row in enumerate(rows):
            at = w * 256 + j * O
            mix_m[at : at + O, :] = jnp.concatenate(row, axis=1)
    hid[0] = jnp.zeros(hid.shape[1:], BF16)
    hid[N // 2 + 1] = jnp.zeros(hid.shape[1:], BF16)

    for c in own:
        c.wait_recv()
    for ri in range(2):
        xt[2 * C : 10 * C, ri * 128 : ri * 128 + 128] = (
            got[:, ri * T : ri * T + T, :].reshape(NF * T, 128).T
        )
    inner = jnp.dot(xt[2 * C : 10 * C, :], fwd_v[...], preferred_element_type=F32).astype(BF16)
    for g in range(NG):
        spec[g, 2 * C : 10 * C, :] = inner[:, g * 128 : g * 128 + 128]

    lane = lax.broadcasted_iota(jnp.int32, (10 * C, 128), 1)
    top = jnp.full((C, 128), jnp.where(has_above, 1.0, 0.0), F32).astype(BF16)
    bottom = jnp.full((C, 128), jnp.where(has_below, 1.0, 0.0), F32).astype(BF16)

    def lift_rows(parts):
        patch = []
        for g in range(NG):
            for lo, n, _ in parts:
                rows = [spec[g, lo + b * C : lo + b * C + n, :] for b in range(3)]
                at = lane[:n]
                patch.append(
                    jnp.where(at < 2 * W, rows[0], jnp.where(at < 4 * W, rows[1], rows[2]))
                )
        patch = jnp.concatenate(patch, axis=0)
        for q in range(G // KB):
            h = jnp.dot(patch, lift_m[:, q * 256 : q * 256 + 256], preferred_element_type=F32)
            h = jnp.maximum(h + lift_bias4, 0.0).astype(BF16)
            at = 0
            for g in range(NG):
                for lo, n, keep in parts:
                    for half in range(2):
                        kp = (g * KB + q) * 2 + half + 1
                        piece = h[at : at + n, half * 128 : half * 128 + 128]
                        hid[kp, lo : lo + n, :] = piece if keep is None else piece * keep
                    at += n

    lift_rows([(2 * C, 6 * C, None)])

    @pl.when(has_above)
    def _():
        for c in down:
            c.wait_recv()

    @pl.when(has_below)
    def _():
        for c in up:
            c.wait_recv()

    quarter = lax.broadcasted_iota(jnp.int32, (NF * T, 128), 1) // (2 * C)
    near = jnp.where(quarter < 2, halo[1].reshape(NF * T, 128), halo[0].reshape(NF * T, 128)).T
    ends_t = jnp.concatenate(
        [
            jnp.concatenate([near[(i + ri) * 2 * C : (i + ri + 1) * 2 * C] for ri in range(2)], axis=1)
            for i in (2, 0)
        ],
        axis=0,
    )
    outer = jnp.dot(ends_t, fwd_v[...], preferred_element_type=F32).astype(BF16)
    for g in range(NG):
        spec[g, : 2 * C, :] = outer[: 2 * C, g * 128 : g * 128 + 128]
        spec[g, 10 * C :, :] = outer[2 * C :, g * 128 : g * 128 + 128]
    lift_rows([(0, C, top), (C, C, None), (8 * C, C, None), (9 * C, C, bottom)])

    blocks = []
    for kp in range(1, N // 2 + 1):
        here = hid[kp]
        beside = jnp.where(lane < O, hid[kp + 1], hid[kp - 1])
        for rp in range(R // 2):
            window = [slice((2 * rp + w) * C, (2 * rp + w + 1) * C) for w in range(4)]
            blocks.append(jnp.concatenate([x[at] for at in window for x in (here, beside)], axis=1))
    mixed = jnp.dot(jnp.concatenate(blocks, axis=0), mix_m[...], preferred_element_type=F32)
    mixed = jnp.maximum(mixed + mix_bias4, 0.0).astype(BF16)
    u = lax.dot_general(
        proj4, mixed, (((1,), (1,)), ((), ())), preferred_element_type=F32
    )
    stay = (lax.broadcasted_iota(jnp.int32, (8, 128), 0) < 4) == (
        lax.broadcasted_iota(jnp.int32, (8, 128), 1) < 64
    )
    update = []
    for i in range(N // 4):
        v = u[:, i * 128 : i * 128 + 128]
        v = jnp.where(stay, v, pltpu.roll(pltpu.roll(v, 4, 0), 64, 1))
        update.append(v + proj_bias4)
    update = jnp.concatenate(update, axis=0).astype(BF16)
    back = jnp.dot(inv_v[...], update, preferred_element_type=F32)
    sent2[...] = back.astype(BF16).reshape(NF, 2 * T, 128)

    second = [
        pltpu.make_async_remote_copy(
            src_ref=sent2.at[p],
            dst_ref=got2.at[f],
            send_sem=send2_sem.at[i],
            recv_sem=recv2_sem.at[i],
            device_id={"frames": p},
            device_id_type=MESH,
        )
        for i, p in enumerate(peers)
    ]
    for c in second:
        c.start()
    got2[f] = sent2[f]
    for c in second:
        c.wait_recv()
    for ri in range(2):
        parts = [got2[i, ri * T : ri * T + T, :].astype(F32) for i in range(NF)]
        for i, part in enumerate(butterfly(parts)):
            row = i % 4 * 2 + i // 4
            at = (ri, pl.ds(row, T, stride=R), slice(None))
            out[at] = part + series_f[at]
    for c in own + second:
        c.wait_send()

    @pl.when(has_below)
    def _():
        for c in down:
            c.wait_send()

    @pl.when(has_above)
    def _():
        for c in up:
            c.wait_send()


def per_device(series, lift_weight, lift_bias, mix_weight, mix_bias, proj_weight, proj_bias):
    n_rows = lax.axis_size("rows")
    args = (
        series,
        jnp.asarray(forward_table()),
        jnp.asarray(inverse_table()),
        jnp.asarray(place_table()),
        lift_weight,
        lift_bias[None],
        mix_weight,
        mix_bias[None],
        proj_weight.T,
        proj_bias[None],
    )
    scratch = [pltpu.VMEM(a.shape, a.dtype) for a in args]
    out = pl.pallas_call(
        functools.partial(kernel, n_rows),
        out_shape=pltpu.VMEM((2, T * R, 128), F32),
        in_specs=[pl.BlockSpec(memory_space=pltpu.HBM)] * len(args),
        out_specs=pl.BlockSpec(memory_space=pltpu.VMEM),
        scratch_shapes=scratch
        + [
            pltpu.VMEM((2, T * R, 128), F32),
            pltpu.VMEM((NF, 2 * T, 128), BF16),
            pltpu.VMEM((NF, T, 128), BF16),
            pltpu.VMEM((NF, 2 * T, 128), BF16),
            pltpu.VMEM((2, NF, T, 128), BF16),
            pltpu.VMEM((12 * C, 256), BF16),
            pltpu.VMEM((NG, 12 * C, 128), BF16),
            pltpu.VMEM((32, 128), F32),
            pltpu.VMEM((8, O), F32),
            pltpu.VMEM((128, G * O), BF16),
            pltpu.VMEM((1024, 256), BF16),
            pltpu.VMEM((N // 2 + 2, 10 * C, 128), BF16),
            pltpu.VMEM((NF, 2 * T, 128), BF16),
            pltpu.VMEM((NF, 2 * T, 128), BF16),
            pltpu.SemaphoreType.DMA((len(args),)),
            pltpu.SemaphoreType.DMA((NF - 1,)),
            pltpu.SemaphoreType.DMA((NF - 1,)),
            pltpu.SemaphoreType.DMA((2, NF)),
            pltpu.SemaphoreType.DMA((2, NF)),
            pltpu.SemaphoreType.DMA((NF - 1,)),
            pltpu.SemaphoreType.DMA((NF - 1,)),
        ],
        compiler_params=pltpu.CompilerParams(
            collective_id=0, has_side_effects=True, vmem_limit_bytes=56 * 1024 * 1024
        ),
    )(*args)
    return jnp.concatenate((out[0], out[1]), axis=1).reshape(T, 1, R, 256)


def solution(mesh):
    return jax.shard_map(
        per_device,
        mesh=mesh,
        in_specs=(P("frames", None, "rows", None), P(), P(), P(), P(), P(), P()),
        out_specs=P("frames", None, "rows", None),
        check_vma=False,
    )
```

```python
import functools
import math

import jax
import jax.numpy as jnp
import ml_dtypes
import numpy as np
from jax import lax
from jax.experimental import pallas as pl
from jax.experimental.pallas import tpu as pltpu
from jax.sharding import PartitionSpec as P

MESH = pl.DeviceIdType.MESH
BF16 = jnp.bfloat16
F32 = jnp.float32

NF = 8
T = 16
N = 128
R = 8
C = 16
O = 64
KB = 4
G = 16
NG = N // G
W = G + 2


def forward_table():
    k = np.arange(N)
    t = np.arange(N)
    angle = (2.0 * math.pi / N * (((k[:, None] - N // 2) * t[None, :]) % N)).astype(np.float32)
    scale = np.float32(1.0 / math.sqrt(N))
    re = (np.cos(angle) * scale).astype(ml_dtypes.bfloat16).astype(np.float32)
    im = (-np.sin(angle) * scale).astype(ml_dtypes.bfloat16).astype(np.float32)
    full = np.zeros((NF, 2, T, NG, 128), np.float32)
    for g in range(NG):
        for w in range(W):
            kk = g * G + w - 1
            if not 0 <= kk < N:
                continue
            a = re[kk].reshape(NF, T)
            b = im[kk].reshape(NF, T)
            for tap in range(3):
                lane = tap * 2 * W + w * 2
                full[:, 0, :, g, lane] = a
                full[:, 1, :, g, lane] = -b
                full[:, 0, :, g, lane + 1] = b
                full[:, 1, :, g, lane + 1] = a
    return full.transpose(1, 0, 2, 3, 4).reshape(2 * NF * T, NG * 128).astype(ml_dtypes.bfloat16)


def inverse_table():
    k = np.arange(N)
    t = np.arange(N)
    angle = (2.0 * math.pi / N * (((k[:, None] - N // 2) * t[None, :]) % N)).astype(np.float32).T
    scale = np.float32(1.0 / math.sqrt(N))
    re = (np.cos(angle) * scale).reshape(NF, T, N)
    im = (np.sin(angle) * scale).reshape(NF, T, N)
    full = np.zeros((NF, 2, T, N, 2), np.float32)
    full[:, 0, :, :, 0] = re
    full[:, 0, :, :, 1] = -im
    full[:, 1, :, :, 0] = im
    full[:, 1, :, :, 1] = re
    return full.reshape(NF * 2 * T, N * 2).astype(ml_dtypes.bfloat16)


def place_table():
    full = np.zeros((G // KB, 128, KB, 32), np.float32)
    for q in range(G // KB):
        for j in range(KB):
            for a in range(3):
                for b in range(3):
                    for i in range(2):
                        full[q, b * 2 * W + (q * KB + j + a) * 2 + i, j, (a * 3 + b) * 2 + i] = 1
    return full.reshape(G // KB, 128, 128).astype(ml_dtypes.bfloat16)


PARTNERS = (5, 7, 3, 1, 4, 6, 2)


def partner(f, m):
    for bit in range(3):
        if m >> bit & 1:
            f = f + (1 << bit) * (1 - 2 * (f // (1 << bit) % 2))
    return f


def butterfly(parts):
    lane = lax.broadcasted_iota(jnp.int32, parts[0].shape, 1)
    for bit in range(3):
        step = 1 << bit
        upper = ((lane >> (4 + bit)) & 1) == 1
        out = list(parts)
        for i in range(8):
            if i & step:
                continue
            lo, hi = parts[i], parts[i + step]
            out[i] = jnp.where(upper, pltpu.roll(hi, 16 * step, 1), lo)
            out[i + step] = jnp.where(upper, hi, pltpu.roll(lo, 128 - 16 * step, 1))
        parts = out
    return parts


def kernel(
    n_rows,
    series,
    fwd,
    inv,
    place,
    lift,
    lift_bias,
    mix,
    mix_bias,
    proj,
    proj_bias,
    out,
    series_v,
    fwd_v,
    inv_v,
    place_v,
    lift_v,
    lift_bias_v,
    mix_v,
    mix_bias_v,
    proj_v,
    proj_bias_v,
    series_f,
    sent,
    edge,
    got,
    halo,
    xt,
    spec,
    taps,
    ends,
    lift_m,
    mix_m,
    hid,
    sent2,
    got2,
    load_sem,
    send_sem,
    recv_sem,
    halo_send_sem,
    halo_recv_sem,
    send2_sem,
    recv2_sem,
):
    f = lax.axis_index("frames")
    r = lax.axis_index("rows")
    above = lax.rem(r + n_rows - 1, n_rows)
    below = lax.rem(r + 1, n_rows)
    has_above = r > 0
    has_below = r < n_rows - 1
    peers = [partner(f, m) for m in PARTNERS]

    loads = [
        pltpu.make_async_copy(a, b, load_sem.at[i])
        for i, (a, b) in enumerate(
            (
                (series, series_v),
                (mix, mix_v),
                (lift, lift_v),
                (place, place_v),
                (fwd, fwd_v),
                (inv, inv_v),
                (lift_bias, lift_bias_v),
                (mix_bias, mix_bias_v),
                (proj, proj_v),
                (proj_bias, proj_bias_v),
            )
        )
    ]
    loads[0].start()

    barrier = pltpu.get_barrier_semaphore()
    for p in peers:
        pl.semaphore_signal(barrier, inc=1, device_id={"frames": p}, device_id_type=MESH)

    for has, near in ((has_above, above), (has_below, below)):

        @pl.when(has)
        def _():
            for p in peers + [f]:
                pl.semaphore_signal(
                    barrier, inc=1, device_id={"frames": p, "rows": near}, device_id_type=MESH
                )

    for c in loads[1:]:
        c.start()

    loads[0].wait()
    for ri in range(2):
        series_f[ri] = series_v[:, 0, :, ri * 128 : ri * 128 + 128].astype(F32).reshape(T * R, 128)
    tiles = [
        butterfly([series_f[ri, pl.ds(i, T, stride=R), :] for i in range(R)]) for ri in range(2)
    ]
    quarter = lax.broadcasted_iota(jnp.int32, (T, 128), 1) // (2 * C)
    for i, (re, im) in enumerate(zip(*tiles)):
        sent[i, :T, :] = re.astype(BF16)
        sent[i, T:, :] = im.astype(BF16)
        low = jnp.where(quarter == 0, re, pltpu.roll(im, 2 * C, 1))
        high = jnp.where(quarter == 2, pltpu.roll(re, 128 - 2 * C, 1), im)
        edge[i] = jnp.where(quarter < 2, low, high).astype(BF16)

    neighbours = jnp.where(has_above, 1, 0) + jnp.where(has_below, 1, 0)
    pl.semaphore_wait(barrier, NF - 1 + NF * neighbours)
    own = [
        pltpu.make_async_remote_copy(
            src_ref=sent.at[p],
            dst_ref=got.at[f],
            send_sem=send_sem.at[i],
            recv_sem=recv_sem.at[i],
            device_id={"frames": p},
            device_id_type=MESH,
        )
        for i, p in enumerate(peers)
    ]
    down, up = (
        [
            pltpu.make_async_remote_copy(
                src_ref=edge.at[p],
                dst_ref=halo.at[side, f],
                send_sem=halo_send_sem.at[side, i],
                recv_sem=halo_recv_sem.at[side, i],
                device_id={"frames": p, "rows": near},
                device_id_type=MESH,
            )
            for i, p in enumerate(peers + [f])
        ]
        for side, near in ((0, below), (1, above))
    )

    for c in own[:3]:
        c.start()

    @pl.when(has_below)
    def _():
        for c in down:
            c.start()

    @pl.when(has_above)
    def _():
        for c in up:
            c.start()

    for c in own[3:]:
        c.start()

    got[f] = sent[f]

    @pl.when(r == 0)
    def _():
        halo[0] = jnp.zeros(halo.shape[1:], BF16)

    @pl.when(r == n_rows - 1)
    def _():
        halo[1] = jnp.zeros(halo.shape[1:], BF16)

    for c in loads[1:]:
        c.wait()
    taps[...] = jnp.zeros(taps.shape, F32)
    for a in range(3):
        for b in range(3):
            taps[(a * 3 + b) * 2 : (a * 3 + b) * 2 + 2, :O] = lift_v[a, b].astype(F32)
    left = taps[...]
    right = pltpu.roll(left, O, 1)
    none = jnp.zeros_like(left)
    lift4 = jnp.concatenate(
        [jnp.concatenate(p, axis=1) for p in ((left, none), (right, none), (none, left), (none, right))],
        axis=0,
    ).astype(BF16)
    for q in range(G // KB):
        lift_m[:, q * 256 : q * 256 + 256] = jnp.dot(
            place_v[q], lift4, preferred_element_type=F32
        ).astype(BF16)
    for k in range(KB):
        ends[k * 2 : k * 2 + 2, :] = proj_v[...].astype(F32)
    proj4 = jnp.concatenate([ends[...]] * KB, axis=1)
    pair = lax.broadcasted_iota(jnp.int32, proj4.shape, 1) // O
    proj4 = jnp.where(
        lax.broadcasted_iota(jnp.int32, proj4.shape, 0) // 2 == pair % 2 * 2 + pair // 2, proj4, 0.0
    ).astype(BF16)
    lift_bias4 = jnp.concatenate([lift_bias_v[...]] * KB, axis=1)
    mix_bias4 = jnp.concatenate([mix_bias_v[...]] * KB, axis=1)
    proj_bias4 = jnp.where(
        lax.broadcasted_iota(jnp.int32, (8, 128), 0) % 2 == 0,
        jnp.broadcast_to(proj_bias_v[:, :1], (8, 128)),
        jnp.broadcast_to(proj_bias_v[:, 1:], (8, 128)),
    )
    zero = jnp.zeros((O, O), BF16)
    for w in range(4):

        def taps_of(a):
            return tuple(mix_v[a, w - r2] if 0 <= w - r2 <= 2 else zero for r2 in range(2))

        blank = (zero, zero)
        rows = (
            taps_of(1) + taps_of(0),
            taps_of(2) + taps_of(1),
            blank + taps_of(2),
            taps_of(0) + blank,
        )
        for j, row in enumerate(rows):
            at = w * 256 + j * O
            mix_m[at : at + O, :] = jnp.concatenate(row, axis=1)
    hid[0] = jnp.zeros(hid.shape[1:], BF16)
    hid[N // 2 + 1] = jnp.zeros(hid.shape[1:], BF16)

    for c in own:
        c.wait_recv()
    for ri in range(2):
        xt[2 * C : 10 * C, ri * 128 : ri * 128 + 128] = (
            got[:, ri * T : ri * T + T, :].reshape(NF * T, 128).T
        )
    inner = jnp.dot(xt[2 * C : 10 * C, :], fwd_v[...], preferred_element_type=F32).astype(BF16)
    for g in range(NG):
        spec[g, 2 * C : 10 * C, :] = inner[:, g * 128 : g * 128 + 128]

    lane = lax.broadcasted_iota(jnp.int32, (10 * C, 128), 1)
    top = jnp.full((C, 128), jnp.where(has_above, 1.0, 0.0), F32).astype(BF16)
    bottom = jnp.full((C, 128), jnp.where(has_below, 1.0, 0.0), F32).astype(BF16)

    def lift_rows(parts):
        patch = []
        for g in range(NG):
            for lo, n, _ in parts:
                rows = [spec[g, lo + b * C : lo + b * C + n, :] for b in range(3)]
                at = lane[:n]
                patch.append(
                    jnp.where(at < 2 * W, rows[0], jnp.where(at < 4 * W, rows[1], rows[2]))
                )
        patch = jnp.concatenate(patch, axis=0)
        for q in range(G // KB):
            h = jnp.dot(patch, lift_m[:, q * 256 : q * 256 + 256], preferred_element_type=F32)
            h = jnp.maximum(h + lift_bias4, 0.0).astype(BF16)
            at = 0
            for g in range(NG):
                for lo, n, keep in parts:
                    for half in range(2):
                        kp = (g * KB + q) * 2 + half + 1
                        piece = h[at : at + n, half * 128 : half * 128 + 128]
                        hid[kp, lo : lo + n, :] = piece if keep is None else piece * keep
                    at += n

    lift_rows([(2 * C, 6 * C, None)])

    @pl.when(has_above)
    def _():
        for c in down:
            c.wait_recv()

    @pl.when(has_below)
    def _():
        for c in up:
            c.wait_recv()

    quarter = lax.broadcasted_iota(jnp.int32, (NF * T, 128), 1) // (2 * C)
    near = jnp.where(quarter < 2, halo[1].reshape(NF * T, 128), halo[0].reshape(NF * T, 128)).T
    ends_t = jnp.concatenate(
        [
            jnp.concatenate([near[(i + ri) * 2 * C : (i + ri + 1) * 2 * C] for ri in range(2)], axis=1)
            for i in (2, 0)
        ],
        axis=0,
    )
    outer = jnp.dot(ends_t, fwd_v[...], preferred_element_type=F32).astype(BF16)
    for g in range(NG):
        spec[g, : 2 * C, :] = outer[: 2 * C, g * 128 : g * 128 + 128]
        spec[g, 10 * C :, :] = outer[2 * C :, g * 128 : g * 128 + 128]
    lift_rows([(0, C, top), (C, C, None), (8 * C, C, None), (9 * C, C, bottom)])

    blocks = []
    for kp in range(1, N // 2 + 1):
        here = hid[kp]
        beside = jnp.where(lane < O, hid[kp + 1], hid[kp - 1])
        for rp in range(R // 2):
            window = [slice((2 * rp + w) * C, (2 * rp + w + 1) * C) for w in range(4)]
            blocks.append(jnp.concatenate([x[at] for at in window for x in (here, beside)], axis=1))
    half = len(blocks) // 2
    mixed = []
    for part in (blocks[:half], blocks[half:]):
        total = jnp.dot(jnp.concatenate(part, axis=0), mix_m[...], preferred_element_type=F32)
        mixed.append(jnp.maximum(total + mix_bias4, 0.0).astype(BF16))
    mixed = jnp.concatenate(mixed, axis=0)
    u = lax.dot_general(
        proj4, mixed, (((1,), (1,)), ((), ())), preferred_element_type=F32
    )
    stay = (lax.broadcasted_iota(jnp.int32, (8, 128), 0) < 4) == (
        lax.broadcasted_iota(jnp.int32, (8, 128), 1) < 64
    )
    update = []
    for i in range(N // 4):
        v = u[:, i * 128 : i * 128 + 128]
        v = jnp.where(stay, v, pltpu.roll(pltpu.roll(v, 4, 0), 64, 1))
        update.append(v + proj_bias4)
    update = jnp.concatenate(update, axis=0).astype(BF16)
    back = jnp.dot(inv_v[...], update, preferred_element_type=F32)
    sent2[...] = back.astype(BF16).reshape(NF, 2 * T, 128)

    second = [
        pltpu.make_async_remote_copy(
            src_ref=sent2.at[p],
            dst_ref=got2.at[f],
            send_sem=send2_sem.at[i],
            recv_sem=recv2_sem.at[i],
            device_id={"frames": p},
            device_id_type=MESH,
        )
        for i, p in enumerate(peers)
    ]
    for c in second:
        c.start()
    got2[f] = sent2[f]
    for c in second:
        c.wait_recv()
    for ri in range(2):
        parts = [got2[i, ri * T : ri * T + T, :].astype(F32) for i in range(NF)]
        for i, part in enumerate(butterfly(parts)):
            row = i % 4 * 2 + i // 4
            at = (ri, pl.ds(row, T, stride=R), slice(None))
            out[at] = part + series_f[at]
    for c in own + second:
        c.wait_send()

    @pl.when(has_below)
    def _():
        for c in down:
            c.wait_send()

    @pl.when(has_above)
    def _():
        for c in up:
            c.wait_send()


def per_device(series, lift_weight, lift_bias, mix_weight, mix_bias, proj_weight, proj_bias):
    n_rows = lax.axis_size("rows")
    args = (
        series,
        jnp.asarray(forward_table()),
        jnp.asarray(inverse_table()),
        jnp.asarray(place_table()),
        lift_weight,
        lift_bias[None],
        mix_weight,
        mix_bias[None],
        proj_weight.T,
        proj_bias[None],
    )
    scratch = [pltpu.VMEM(a.shape, a.dtype) for a in args]
    out = pl.pallas_call(
        functools.partial(kernel, n_rows),
        out_shape=pltpu.VMEM((2, T * R, 128), F32),
        in_specs=[pl.BlockSpec(memory_space=pltpu.HBM)] * len(args),
        out_specs=pl.BlockSpec(memory_space=pltpu.VMEM),
        scratch_shapes=scratch
        + [
            pltpu.VMEM((2, T * R, 128), F32),
            pltpu.VMEM((NF, 2 * T, 128), BF16),
            pltpu.VMEM((NF, T, 128), BF16),
            pltpu.VMEM((NF, 2 * T, 128), BF16),
            pltpu.VMEM((2, NF, T, 128), BF16),
            pltpu.VMEM((12 * C, 256), BF16),
            pltpu.VMEM((NG, 12 * C, 128), BF16),
            pltpu.VMEM((32, 128), F32),
            pltpu.VMEM((8, O), F32),
            pltpu.VMEM((128, G * O), BF16),
            pltpu.VMEM((1024, 256), BF16),
            pltpu.VMEM((N // 2 + 2, 10 * C, 128), BF16),
            pltpu.VMEM((NF, 2 * T, 128), BF16),
            pltpu.VMEM((NF, 2 * T, 128), BF16),
            pltpu.SemaphoreType.DMA((len(args),)),
            pltpu.SemaphoreType.DMA((NF - 1,)),
            pltpu.SemaphoreType.DMA((NF - 1,)),
            pltpu.SemaphoreType.DMA((2, NF)),
            pltpu.SemaphoreType.DMA((2, NF)),
            pltpu.SemaphoreType.DMA((NF - 1,)),
            pltpu.SemaphoreType.DMA((NF - 1,)),
        ],
        compiler_params=pltpu.CompilerParams(
            collective_id=0, has_side_effects=True, vmem_limit_bytes=56 * 1024 * 1024
        ),
    )(*args)
    return jnp.concatenate((out[0], out[1]), axis=1).reshape(T, 1, R, 256)


def solution(mesh):
    return jax.shard_map(
        per_device,
        mesh=mesh,
        in_specs=(P("frames", None, "rows", None), P(), P(), P(), P(), P(), P()),
        out_specs=P("frames", None, "rows", None),
        check_vma=False,
    )
```

```python
import functools
import math

import jax
import jax.numpy as jnp
import ml_dtypes
import numpy as np
from jax import lax
from jax.experimental import pallas as pl
from jax.experimental.pallas import tpu as pltpu
from jax.sharding import PartitionSpec as P

MESH = pl.DeviceIdType.MESH
BF16 = jnp.bfloat16
F32 = jnp.float32

NF = 8
T = 16
N = 128
R = 8
C = 16
O = 64
KB = 4
G = 16
NG = N // G
W = G + 2


def forward_table():
    k = np.arange(N)
    t = np.arange(N)
    angle = (2.0 * math.pi / N * (((k[:, None] - N // 2) * t[None, :]) % N)).astype(np.float32)
    scale = np.float32(1.0 / math.sqrt(N))
    re = (np.cos(angle) * scale).astype(ml_dtypes.bfloat16).astype(np.float32)
    im = (-np.sin(angle) * scale).astype(ml_dtypes.bfloat16).astype(np.float32)
    full = np.zeros((NF, 2, T, NG, 128), np.float32)
    for g in range(NG):
        for w in range(W):
            kk = g * G + w - 1
            if not 0 <= kk < N:
                continue
            a = re[kk].reshape(NF, T)
            b = im[kk].reshape(NF, T)
            for tap in range(3):
                lane = tap * 2 * W + w * 2
                full[:, 0, :, g, lane] = a
                full[:, 1, :, g, lane] = -b
                full[:, 0, :, g, lane + 1] = b
                full[:, 1, :, g, lane + 1] = a
    return full.transpose(1, 0, 2, 3, 4).reshape(2 * NF * T, NG * 128).astype(ml_dtypes.bfloat16)


def inverse_table():
    k = np.arange(N)
    t = np.arange(N)
    angle = (2.0 * math.pi / N * (((k[:, None] - N // 2) * t[None, :]) % N)).astype(np.float32).T
    scale = np.float32(1.0 / math.sqrt(N))
    re = (np.cos(angle) * scale).reshape(NF, T, N)
    im = (np.sin(angle) * scale).reshape(NF, T, N)
    full = np.zeros((NF, 2, T, N, 2), np.float32)
    full[:, 0, :, :, 0] = re
    full[:, 0, :, :, 1] = -im
    full[:, 1, :, :, 0] = im
    full[:, 1, :, :, 1] = re
    return full.reshape(NF * 2 * T, N * 2).astype(ml_dtypes.bfloat16)


def place_table():
    full = np.zeros((G // KB, 128, KB, 32), np.float32)
    for q in range(G // KB):
        for j in range(KB):
            for a in range(3):
                for b in range(3):
                    for i in range(2):
                        full[q, b * 2 * W + (q * KB + j + a) * 2 + i, j, (a * 3 + b) * 2 + i] = 1
    return full.reshape(G // KB, 128, 128).astype(ml_dtypes.bfloat16)


PARTNERS = (5, 7, 3, 1, 4, 6, 2)


def partner(f, m):
    for bit in range(3):
        if m >> bit & 1:
            f = f + (1 << bit) * (1 - 2 * (f // (1 << bit) % 2))
    return f


def butterfly(parts):
    lane = lax.broadcasted_iota(jnp.int32, parts[0].shape, 1)
    for bit in range(3):
        step = 1 << bit
        upper = ((lane >> (4 + bit)) & 1) == 1
        out = list(parts)
        for i in range(8):
            if i & step:
                continue
            lo, hi = parts[i], parts[i + step]
            out[i] = jnp.where(upper, pltpu.roll(hi, 16 * step, 1), lo)
            out[i + step] = jnp.where(upper, hi, pltpu.roll(lo, 128 - 16 * step, 1))
        parts = out
    return parts


def kernel(
    n_rows,
    series,
    fwd,
    inv,
    place,
    lift,
    lift_bias,
    mix,
    mix_bias,
    proj,
    proj_bias,
    out,
    series_v,
    fwd_v,
    inv_v,
    place_v,
    lift_v,
    lift_bias_v,
    mix_v,
    mix_bias_v,
    proj_v,
    proj_bias_v,
    series_f,
    sent,
    edge,
    got,
    halo,
    xt,
    spec,
    taps,
    ends,
    lift_m,
    mix_m,
    hid,
    sent2,
    got2,
    load_sem,
    send_sem,
    recv_sem,
    halo_send_sem,
    halo_recv_sem,
    send2_sem,
    recv2_sem,
):
    f = lax.axis_index("frames")
    r = lax.axis_index("rows")
    above = lax.rem(r + n_rows - 1, n_rows)
    below = lax.rem(r + 1, n_rows)
    has_above = r > 0
    has_below = r < n_rows - 1
    peers = [partner(f, m) for m in PARTNERS]

    loads = [
        pltpu.make_async_copy(a, b, load_sem.at[i])
        for i, (a, b) in enumerate(
            (
                (series, series_v),
                (mix, mix_v),
                (lift, lift_v),
                (place, place_v),
                (fwd, fwd_v),
                (inv, inv_v),
                (lift_bias, lift_bias_v),
                (mix_bias, mix_bias_v),
                (proj, proj_v),
                (proj_bias, proj_bias_v),
            )
        )
    ]
    loads[0].start()

    barrier = pltpu.get_barrier_semaphore()
    for p in peers:
        pl.semaphore_signal(barrier, inc=1, device_id={"frames": p}, device_id_type=MESH)

    for has, near in ((has_above, above), (has_below, below)):

        @pl.when(has)
        def _():
            for p in peers + [f]:
                pl.semaphore_signal(
                    barrier, inc=1, device_id={"frames": p, "rows": near}, device_id_type=MESH
                )

    for c in loads[1:]:
        c.start()

    loads[0].wait()
    for ri in range(2):
        series_f[ri] = series_v[:, 0, :, ri * 128 : ri * 128 + 128].astype(F32).reshape(T * R, 128)
    tiles = [
        butterfly([series_f[ri, pl.ds(i, T, stride=R), :] for i in range(R)]) for ri in range(2)
    ]
    quarter = lax.broadcasted_iota(jnp.int32, (T, 128), 1) // (2 * C)
    for i, (re, im) in enumerate(zip(*tiles)):
        sent[i, :T, :] = re.astype(BF16)
        sent[i, T:, :] = im.astype(BF16)
        low = jnp.where(quarter == 0, re, pltpu.roll(im, 2 * C, 1))
        high = jnp.where(quarter == 2, pltpu.roll(re, 128 - 2 * C, 1), im)
        edge[i] = jnp.where(quarter < 2, low, high).astype(BF16)

    neighbours = jnp.where(has_above, 1, 0) + jnp.where(has_below, 1, 0)
    pl.semaphore_wait(barrier, NF - 1 + NF * neighbours)
    own = [
        pltpu.make_async_remote_copy(
            src_ref=sent.at[p],
            dst_ref=got.at[f],
            send_sem=send_sem.at[i],
            recv_sem=recv_sem.at[i],
            device_id={"frames": p},
            device_id_type=MESH,
        )
        for i, p in enumerate(peers)
    ]
    down, up = (
        [
            pltpu.make_async_remote_copy(
                src_ref=edge.at[p],
                dst_ref=halo.at[side, f],
                send_sem=halo_send_sem.at[side, i],
                recv_sem=halo_recv_sem.at[side, i],
                device_id={"frames": p, "rows": near},
                device_id_type=MESH,
            )
            for i, p in enumerate(peers + [f])
        ]
        for side, near in ((0, below), (1, above))
    )

    for c in own[:3]:
        c.start()

    @pl.when(has_below)
    def _():
        for c in down:
            c.start()

    @pl.when(has_above)
    def _():
        for c in up:
            c.start()

    for c in own[3:]:
        c.start()

    got[f] = sent[f]

    @pl.when(r == 0)
    def _():
        halo[0] = jnp.zeros(halo.shape[1:], BF16)

    @pl.when(r == n_rows - 1)
    def _():
        halo[1] = jnp.zeros(halo.shape[1:], BF16)

    for c in loads[1:]:
        c.wait()
    taps[...] = jnp.zeros(taps.shape, F32)
    for a in range(3):
        for b in range(3):
            taps[(a * 3 + b) * 2 : (a * 3 + b) * 2 + 2, :O] = lift_v[a, b].astype(F32)
    left = taps[...]
    right = pltpu.roll(left, O, 1)
    none = jnp.zeros_like(left)
    lift4 = jnp.concatenate(
        [jnp.concatenate(p, axis=1) for p in ((left, none), (right, none), (none, left), (none, right))],
        axis=0,
    ).astype(BF16)
    for q in range(G // KB):
        lift_m[:, q * 256 : q * 256 + 256] = jnp.dot(
            place_v[q], lift4, preferred_element_type=F32
        ).astype(BF16)
    for k in range(KB):
        ends[k * 2 : k * 2 + 2, :] = proj_v[...].astype(F32)
    proj4 = jnp.concatenate([ends[...]] * KB, axis=1)
    pair = lax.broadcasted_iota(jnp.int32, proj4.shape, 1) // O
    proj4 = jnp.where(
        lax.broadcasted_iota(jnp.int32, proj4.shape, 0) // 2 == pair % 2 * 2 + pair // 2, proj4, 0.0
    ).astype(BF16)
    lift_bias4 = jnp.concatenate([lift_bias_v[...]] * KB, axis=1)
    mix_bias4 = jnp.concatenate([mix_bias_v[...]] * KB, axis=1)
    proj_bias4 = jnp.where(
        lax.broadcasted_iota(jnp.int32, (8, 128), 0) % 2 == 0,
        jnp.broadcast_to(proj_bias_v[:, :1], (8, 128)),
        jnp.broadcast_to(proj_bias_v[:, 1:], (8, 128)),
    )
    zero = jnp.zeros((O, O), BF16)
    for w in range(4):

        def taps_of(a):
            return tuple(mix_v[a, w - r2] if 0 <= w - r2 <= 2 else zero for r2 in range(2))

        blank = (zero, zero)
        rows = (
            taps_of(1) + taps_of(0),
            taps_of(2) + taps_of(1),
            blank + taps_of(2),
            taps_of(0) + blank,
        )
        for j, row in enumerate(rows):
            at = w * 256 + j * O
            mix_m[at : at + O, :] = jnp.concatenate(row, axis=1)
    hid[0] = jnp.zeros(hid.shape[1:], BF16)
    hid[N // 2 + 1] = jnp.zeros(hid.shape[1:], BF16)

    for c in own:
        c.wait_recv()
    for ri in range(2):
        xt[2 * C : 10 * C, ri * 128 : ri * 128 + 128] = (
            got[:, ri * T : ri * T + T, :].reshape(NF * T, 128).T
        )
    inner = jnp.dot(xt[2 * C : 10 * C, :], fwd_v[...], preferred_element_type=F32).astype(BF16)
    for g in range(NG):
        spec[g, 2 * C : 10 * C, :] = inner[:, g * 128 : g * 128 + 128]

    lane = lax.broadcasted_iota(jnp.int32, (10 * C, 128), 1)
    top = jnp.full((C, 128), jnp.where(has_above, 1.0, 0.0), F32).astype(BF16)
    bottom = jnp.full((C, 128), jnp.where(has_below, 1.0, 0.0), F32).astype(BF16)

    def lift_rows(parts):
        patch = []
        for g in range(NG):
            for lo, n, _ in parts:
                rows = [spec[g, lo + b * C : lo + b * C + n, :] for b in range(3)]
                at = lane[:n]
                patch.append(
                    jnp.where(at < 2 * W, rows[0], jnp.where(at < 4 * W, rows[1], rows[2]))
                )
        patch = jnp.concatenate(patch, axis=0)
        for q in range(G // KB):
            h = jnp.dot(patch, lift_m[:, q * 256 : q * 256 + 256], preferred_element_type=F32)
            h = jnp.maximum(h + lift_bias4, 0.0).astype(BF16)
            at = 0
            for g in range(NG):
                for lo, n, keep in parts:
                    for half in range(2):
                        kp = (g * KB + q) * 2 + half + 1
                        piece = h[at : at + n, half * 128 : half * 128 + 128]
                        hid[kp, lo : lo + n, :] = piece if keep is None else piece * keep
                    at += n

    lift_rows([(2 * C, 6 * C, None)])

    @pl.when(has_above)
    def _():
        for c in down:
            c.wait_recv()

    @pl.when(has_below)
    def _():
        for c in up:
            c.wait_recv()

    quarter = lax.broadcasted_iota(jnp.int32, (NF * T, 128), 1) // (2 * C)
    near = jnp.where(quarter < 2, halo[1].reshape(NF * T, 128), halo[0].reshape(NF * T, 128)).T
    ends_t = jnp.concatenate(
        [
            jnp.concatenate([near[(i + ri) * 2 * C : (i + ri + 1) * 2 * C] for ri in range(2)], axis=1)
            for i in (2, 0)
        ],
        axis=0,
    )
    outer = jnp.dot(ends_t, fwd_v[...], preferred_element_type=F32).astype(BF16)
    for g in range(NG):
        spec[g, : 2 * C, :] = outer[: 2 * C, g * 128 : g * 128 + 128]
        spec[g, 10 * C :, :] = outer[2 * C :, g * 128 : g * 128 + 128]
    lift_rows([(0, C, top), (C, C, None), (8 * C, C, None), (9 * C, C, bottom)])

    blocks = []
    for kp in range(1, N // 2 + 1):
        here = hid[kp]
        beside = jnp.where(lane < O, hid[kp + 1], hid[kp - 1])
        for rp in range(R // 2):
            window = [slice((2 * rp + w) * C, (2 * rp + w + 1) * C) for w in range(4)]
            blocks.append(jnp.concatenate([x[at] for at in window for x in (here, beside)], axis=1))
    size = len(blocks) // 4
    mixed = []
    for part in (blocks[i * size : (i + 1) * size] for i in range(4)):
        total = jnp.dot(jnp.concatenate(part, axis=0), mix_m[...], preferred_element_type=F32)
        mixed.append(jnp.maximum(total + mix_bias4, 0.0).astype(BF16))
    mixed = jnp.concatenate(mixed, axis=0)
    u = lax.dot_general(
        proj4, mixed, (((1,), (1,)), ((), ())), preferred_element_type=F32
    )
    stay = (lax.broadcasted_iota(jnp.int32, (8, 128), 0) < 4) == (
        lax.broadcasted_iota(jnp.int32, (8, 128), 1) < 64
    )
    update = []
    for i in range(N // 4):
        v = u[:, i * 128 : i * 128 + 128]
        v = jnp.where(stay, v, pltpu.roll(pltpu.roll(v, 4, 0), 64, 1))
        update.append(v + proj_bias4)
    update = jnp.concatenate(update, axis=0).astype(BF16)
    back = jnp.dot(inv_v[...], update, preferred_element_type=F32)
    sent2[...] = back.astype(BF16).reshape(NF, 2 * T, 128)

    second = [
        pltpu.make_async_remote_copy(
            src_ref=sent2.at[p],
            dst_ref=got2.at[f],
            send_sem=send2_sem.at[i],
            recv_sem=recv2_sem.at[i],
            device_id={"frames": p},
            device_id_type=MESH,
        )
        for i, p in enumerate(peers)
    ]
    for c in second:
        c.start()
    got2[f] = sent2[f]
    for c in second:
        c.wait_recv()
    for ri in range(2):
        parts = [got2[i, ri * T : ri * T + T, :].astype(F32) for i in range(NF)]
        for i, part in enumerate(butterfly(parts)):
            row = i % 4 * 2 + i // 4
            at = (ri, pl.ds(row, T, stride=R), slice(None))
            out[at] = part + series_f[at]
    for c in own + second:
        c.wait_send()

    @pl.when(has_below)
    def _():
        for c in down:
            c.wait_send()

    @pl.when(has_above)
    def _():
        for c in up:
            c.wait_send()


def per_device(series, lift_weight, lift_bias, mix_weight, mix_bias, proj_weight, proj_bias):
    n_rows = lax.axis_size("rows")
    args = (
        series,
        jnp.asarray(forward_table()),
        jnp.asarray(inverse_table()),
        jnp.asarray(place_table()),
        lift_weight,
        lift_bias[None],
        mix_weight,
        mix_bias[None],
        proj_weight.T,
        proj_bias[None],
    )
    scratch = [pltpu.VMEM(a.shape, a.dtype) for a in args]
    out = pl.pallas_call(
        functools.partial(kernel, n_rows),
        out_shape=pltpu.VMEM((2, T * R, 128), F32),
        in_specs=[pl.BlockSpec(memory_space=pltpu.HBM)] * len(args),
        out_specs=pl.BlockSpec(memory_space=pltpu.VMEM),
        scratch_shapes=scratch
        + [
            pltpu.VMEM((2, T * R, 128), F32),
            pltpu.VMEM((NF, 2 * T, 128), BF16),
            pltpu.VMEM((NF, T, 128), BF16),
            pltpu.VMEM((NF, 2 * T, 128), BF16),
            pltpu.VMEM((2, NF, T, 128), BF16),
            pltpu.VMEM((12 * C, 256), BF16),
            pltpu.VMEM((NG, 12 * C, 128), BF16),
            pltpu.VMEM((32, 128), F32),
            pltpu.VMEM((8, O), F32),
            pltpu.VMEM((128, G * O), BF16),
            pltpu.VMEM((1024, 256), BF16),
            pltpu.VMEM((N // 2 + 2, 10 * C, 128), BF16),
            pltpu.VMEM((NF, 2 * T, 128), BF16),
            pltpu.VMEM((NF, 2 * T, 128), BF16),
            pltpu.SemaphoreType.DMA((len(args),)),
            pltpu.SemaphoreType.DMA((NF - 1,)),
            pltpu.SemaphoreType.DMA((NF - 1,)),
            pltpu.SemaphoreType.DMA((2, NF)),
            pltpu.SemaphoreType.DMA((2, NF)),
            pltpu.SemaphoreType.DMA((NF - 1,)),
            pltpu.SemaphoreType.DMA((NF - 1,)),
        ],
        compiler_params=pltpu.CompilerParams(
            collective_id=0, has_side_effects=True, vmem_limit_bytes=56 * 1024 * 1024
        ),
    )(*args)
    return jnp.concatenate((out[0], out[1]), axis=1).reshape(T, 1, R, 256)


def solution(mesh):
    return jax.shard_map(
        per_device,
        mesh=mesh,
        in_specs=(P("frames", None, "rows", None), P(), P(), P(), P(), P(), P()),
        out_specs=P("frames", None, "rows", None),
        check_vma=False,
    )
```

```python
import functools
import math

import jax
import jax.numpy as jnp
import ml_dtypes
import numpy as np
from jax import lax
from jax.experimental import pallas as pl
from jax.experimental.pallas import tpu as pltpu
from jax.sharding import PartitionSpec as P

MESH = pl.DeviceIdType.MESH
BF16 = jnp.bfloat16
F32 = jnp.float32

NF = 8
T = 16
N = 128
R = 8
C = 16
O = 64
KB = 4
G = 16
NG = N // G
W = G + 2


def forward_table():
    k = np.arange(N)
    t = np.arange(N)
    angle = (2.0 * math.pi / N * (((k[:, None] - N // 2) * t[None, :]) % N)).astype(np.float32)
    scale = np.float32(1.0 / math.sqrt(N))
    re = (np.cos(angle) * scale).astype(ml_dtypes.bfloat16).astype(np.float32)
    im = (-np.sin(angle) * scale).astype(ml_dtypes.bfloat16).astype(np.float32)
    full = np.zeros((NF, 2, T, NG, 128), np.float32)
    for g in range(NG):
        for w in range(W):
            kk = g * G + w - 1
            if not 0 <= kk < N:
                continue
            a = re[kk].reshape(NF, T)
            b = im[kk].reshape(NF, T)
            for tap in range(3):
                lane = tap * 2 * W + w * 2
                full[:, 0, :, g, lane] = a
                full[:, 1, :, g, lane] = -b
                full[:, 0, :, g, lane + 1] = b
                full[:, 1, :, g, lane + 1] = a
    return full.transpose(1, 0, 2, 3, 4).reshape(2 * NF * T, NG * 128).astype(ml_dtypes.bfloat16)


def inverse_table():
    k = np.arange(N)
    t = np.arange(N)
    angle = (2.0 * math.pi / N * (((k[:, None] - N // 2) * t[None, :]) % N)).astype(np.float32).T
    scale = np.float32(1.0 / math.sqrt(N))
    re = (np.cos(angle) * scale).reshape(NF, T, N)
    im = (np.sin(angle) * scale).reshape(NF, T, N)
    full = np.zeros((NF, 2, T, N, 2), np.float32)
    full[:, 0, :, :, 0] = re
    full[:, 0, :, :, 1] = -im
    full[:, 1, :, :, 0] = im
    full[:, 1, :, :, 1] = re
    return full.reshape(NF * 2 * T, N * 2).astype(ml_dtypes.bfloat16)


def place_table():
    full = np.zeros((G // KB, 128, KB, 32), np.float32)
    for q in range(G // KB):
        for j in range(KB):
            for a in range(3):
                for b in range(3):
                    for i in range(2):
                        full[q, b * 2 * W + (q * KB + j + a) * 2 + i, j, (a * 3 + b) * 2 + i] = 1
    return full.reshape(G // KB, 128, 128).astype(ml_dtypes.bfloat16)


PARTNERS = (5, 7, 3, 1, 4, 6, 2)


def partner(f, m):
    for bit in range(3):
        if m >> bit & 1:
            f = f + (1 << bit) * (1 - 2 * (f // (1 << bit) % 2))
    return f


def butterfly(parts):
    lane = lax.broadcasted_iota(jnp.int32, parts[0].shape, 1)
    for bit in range(3):
        step = 1 << bit
        upper = ((lane >> (4 + bit)) & 1) == 1
        out = list(parts)
        for i in range(8):
            if i & step:
                continue
            lo, hi = parts[i], parts[i + step]
            out[i] = jnp.where(upper, pltpu.roll(hi, 16 * step, 1), lo)
            out[i + step] = jnp.where(upper, hi, pltpu.roll(lo, 128 - 16 * step, 1))
        parts = out
    return parts


def kernel(
    n_rows,
    series,
    fwd,
    inv,
    place,
    lift,
    lift_bias,
    mix,
    mix_bias,
    proj,
    proj_bias,
    out,
    series_v,
    fwd_v,
    inv_v,
    place_v,
    lift_v,
    lift_bias_v,
    mix_v,
    mix_bias_v,
    proj_v,
    proj_bias_v,
    series_f,
    sent,
    edge,
    got,
    halo,
    xt,
    spec,
    taps,
    ends,
    lift_m,
    mix_m,
    hid,
    sent2,
    got2,
    load_sem,
    send_sem,
    recv_sem,
    halo_send_sem,
    halo_recv_sem,
    send2_sem,
    recv2_sem,
):
    f = lax.axis_index("frames")
    r = lax.axis_index("rows")
    above = lax.rem(r + n_rows - 1, n_rows)
    below = lax.rem(r + 1, n_rows)
    has_above = r > 0
    has_below = r < n_rows - 1
    peers = [partner(f, m) for m in PARTNERS]

    loads = [
        pltpu.make_async_copy(a, b, load_sem.at[i])
        for i, (a, b) in enumerate(
            (
                (series, series_v),
                (mix, mix_v),
                (lift, lift_v),
                (place, place_v),
                (fwd, fwd_v),
                (inv, inv_v),
                (lift_bias, lift_bias_v),
                (mix_bias, mix_bias_v),
                (proj, proj_v),
                (proj_bias, proj_bias_v),
            )
        )
    ]
    loads[0].start()

    barrier = pltpu.get_barrier_semaphore()
    for p in peers:
        pl.semaphore_signal(barrier, inc=1, device_id={"frames": p}, device_id_type=MESH)

    for has, near in ((has_above, above), (has_below, below)):

        @pl.when(has)
        def _():
            for p in peers + [f]:
                pl.semaphore_signal(
                    barrier, inc=1, device_id={"frames": p, "rows": near}, device_id_type=MESH
                )

    for c in loads[1:]:
        c.start()

    loads[0].wait()
    for ri in range(2):
        series_f[ri] = series_v[:, 0, :, ri * 128 : ri * 128 + 128].astype(F32).reshape(T * R, 128)
    tiles = [
        butterfly([series_f[ri, pl.ds(i, T, stride=R), :] for i in range(R)]) for ri in range(2)
    ]
    quarter = lax.broadcasted_iota(jnp.int32, (T, 128), 1) // (2 * C)
    for i, (re, im) in enumerate(zip(*tiles)):
        sent[i, :T, :] = re.astype(BF16)
        sent[i, T:, :] = im.astype(BF16)
        low = jnp.where(quarter == 0, re, pltpu.roll(im, 2 * C, 1))
        high = jnp.where(quarter == 2, pltpu.roll(re, 128 - 2 * C, 1), im)
        edge[i] = jnp.where(quarter < 2, low, high).astype(BF16)

    neighbours = jnp.where(has_above, 1, 0) + jnp.where(has_below, 1, 0)
    pl.semaphore_wait(barrier, NF - 1 + NF * neighbours)
    own = [
        pltpu.make_async_remote_copy(
            src_ref=sent.at[p],
            dst_ref=got.at[f],
            send_sem=send_sem.at[i],
            recv_sem=recv_sem.at[i],
            device_id={"frames": p},
            device_id_type=MESH,
        )
        for i, p in enumerate(peers)
    ]
    down, up = (
        [
            pltpu.make_async_remote_copy(
                src_ref=edge.at[p],
                dst_ref=halo.at[side, f],
                send_sem=halo_send_sem.at[side, i],
                recv_sem=halo_recv_sem.at[side, i],
                device_id={"frames": p, "rows": near},
                device_id_type=MESH,
            )
            for i, p in enumerate(peers + [f])
        ]
        for side, near in ((0, below), (1, above))
    )

    for c in own[:3]:
        c.start()

    @pl.when(has_below)
    def _():
        for c in down:
            c.start()

    @pl.when(has_above)
    def _():
        for c in up:
            c.start()

    for c in own[3:]:
        c.start()

    got[f] = sent[f]

    @pl.when(r == 0)
    def _():
        halo[0] = jnp.zeros(halo.shape[1:], BF16)

    @pl.when(r == n_rows - 1)
    def _():
        halo[1] = jnp.zeros(halo.shape[1:], BF16)

    for c in loads[1:]:
        c.wait()
    taps[...] = jnp.zeros(taps.shape, F32)
    for a in range(3):
        for b in range(3):
            taps[(a * 3 + b) * 2 : (a * 3 + b) * 2 + 2, :O] = lift_v[a, b].astype(F32)
    left = taps[...]
    right = pltpu.roll(left, O, 1)
    none = jnp.zeros_like(left)
    lift4 = jnp.concatenate(
        [jnp.concatenate(p, axis=1) for p in ((left, none), (right, none), (none, left), (none, right))],
        axis=0,
    ).astype(BF16)
    for q in range(G // KB):
        lift_m[:, q * 256 : q * 256 + 256] = jnp.dot(
            place_v[q], lift4, preferred_element_type=F32
        ).astype(BF16)
    for k in range(KB):
        ends[k * 2 : k * 2 + 2, :] = proj_v[...].astype(F32)
    proj4 = jnp.concatenate([ends[...]] * KB, axis=1)
    pair = lax.broadcasted_iota(jnp.int32, proj4.shape, 1) // O
    proj4 = jnp.where(
        lax.broadcasted_iota(jnp.int32, proj4.shape, 0) // 2 == pair % 2 * 2 + pair // 2, proj4, 0.0
    ).astype(BF16)
    lift_bias4 = jnp.concatenate([lift_bias_v[...]] * KB, axis=1)
    mix_bias4 = jnp.concatenate([mix_bias_v[...]] * KB, axis=1)
    proj_bias4 = jnp.where(
        lax.broadcasted_iota(jnp.int32, (8, 128), 0) % 2 == 0,
        jnp.broadcast_to(proj_bias_v[:, :1], (8, 128)),
        jnp.broadcast_to(proj_bias_v[:, 1:], (8, 128)),
    )
    zero = jnp.zeros((O, O), BF16)
    for w in range(4):

        def taps_of(a):
            return tuple(mix_v[a, w - r2] if 0 <= w - r2 <= 2 else zero for r2 in range(2))

        blank = (zero, zero)
        rows = (
            taps_of(1) + taps_of(0),
            taps_of(2) + taps_of(1),
            blank + taps_of(2),
            taps_of(0) + blank,
        )
        for j, row in enumerate(rows):
            at = w * 256 + j * O
            mix_m[at : at + O, :] = jnp.concatenate(row, axis=1)
    hid[0] = jnp.zeros(hid.shape[1:], BF16)
    hid[N // 2 + 1] = jnp.zeros(hid.shape[1:], BF16)

    for c in own:
        c.wait_recv()
    for ri in range(2):
        xt[2 * C : 10 * C, ri * 128 : ri * 128 + 128] = (
            got[:, ri * T : ri * T + T, :].reshape(NF * T, 128).T
        )
    inner = jnp.dot(xt[2 * C : 10 * C, :], fwd_v[...], preferred_element_type=F32).astype(BF16)
    for g in range(NG):
        spec[g, 2 * C : 10 * C, :] = inner[:, g * 128 : g * 128 + 128]

    lane = lax.broadcasted_iota(jnp.int32, (10 * C, 128), 1)
    top = jnp.full((C, 128), jnp.where(has_above, 1.0, 0.0), F32).astype(BF16)
    bottom = jnp.full((C, 128), jnp.where(has_below, 1.0, 0.0), F32).astype(BF16)

    def lift_rows(parts):
        patch = []
        for g in range(NG):
            for lo, n, _ in parts:
                rows = [spec[g, lo + b * C : lo + b * C + n, :] for b in range(3)]
                at = lane[:n]
                patch.append(
                    jnp.where(at < 2 * W, rows[0], jnp.where(at < 4 * W, rows[1], rows[2]))
                )
        patch = jnp.concatenate(patch, axis=0)
        for q in range(G // KB):
            h = jnp.dot(patch, lift_m[:, q * 256 : q * 256 + 256], preferred_element_type=F32)
            h = jnp.maximum(h + lift_bias4, 0.0).astype(BF16)
            at = 0
            for g in range(NG):
                for lo, n, keep in parts:
                    for half in range(2):
                        kp = (g * KB + q) * 2 + half + 1
                        piece = h[at : at + n, half * 128 : half * 128 + 128]
                        hid[kp, lo : lo + n, :] = piece if keep is None else piece * keep
                    at += n

    lift_rows([(2 * C, 6 * C, None)])

    @pl.when(has_above)
    def _():
        for c in down:
            c.wait_recv()

    @pl.when(has_below)
    def _():
        for c in up:
            c.wait_recv()

    quarter = lax.broadcasted_iota(jnp.int32, (NF * T, 128), 1) // (2 * C)
    near = jnp.where(quarter < 2, halo[1].reshape(NF * T, 128), halo[0].reshape(NF * T, 128)).T
    ends_t = jnp.concatenate(
        [
            jnp.concatenate([near[(i + ri) * 2 * C : (i + ri + 1) * 2 * C] for ri in range(2)], axis=1)
            for i in (2, 0)
        ],
        axis=0,
    )
    outer = jnp.dot(ends_t, fwd_v[...], preferred_element_type=F32).astype(BF16)
    for g in range(NG):
        spec[g, : 2 * C, :] = outer[: 2 * C, g * 128 : g * 128 + 128]
        spec[g, 10 * C :, :] = outer[2 * C :, g * 128 : g * 128 + 128]
    lift_rows([(0, C, top), (C, C, None), (8 * C, C, None), (9 * C, C, bottom)])

    blocks = []
    for kp in range(1, N // 2 + 1):
        here = hid[kp]
        beside = jnp.where(lane < O, hid[kp + 1], hid[kp - 1])
        for rp in range(R // 2):
            window = [slice((2 * rp + w) * C, (2 * rp + w + 1) * C) for w in range(4)]
            blocks.append(jnp.concatenate([x[at] for at in window for x in (here, beside)], axis=1))
    size = len(blocks) // 8
    mixed = []
    for part in (blocks[i * size : (i + 1) * size] for i in range(8)):
        total = jnp.dot(jnp.concatenate(part, axis=0), mix_m[...], preferred_element_type=F32)
        mixed.append(jnp.maximum(total + mix_bias4, 0.0).astype(BF16))
    mixed = jnp.concatenate(mixed, axis=0)
    u = lax.dot_general(
        proj4, mixed, (((1,), (1,)), ((), ())), preferred_element_type=F32
    )
    stay = (lax.broadcasted_iota(jnp.int32, (8, 128), 0) < 4) == (
        lax.broadcasted_iota(jnp.int32, (8, 128), 1) < 64
    )
    update = []
    for i in range(N // 4):
        v = u[:, i * 128 : i * 128 + 128]
        v = jnp.where(stay, v, pltpu.roll(pltpu.roll(v, 4, 0), 64, 1))
        update.append(v + proj_bias4)
    update = jnp.concatenate(update, axis=0).astype(BF16)
    back = jnp.dot(inv_v[...], update, preferred_element_type=F32)
    sent2[...] = back.astype(BF16).reshape(NF, 2 * T, 128)

    second = [
        pltpu.make_async_remote_copy(
            src_ref=sent2.at[p],
            dst_ref=got2.at[f],
            send_sem=send2_sem.at[i],
            recv_sem=recv2_sem.at[i],
            device_id={"frames": p},
            device_id_type=MESH,
        )
        for i, p in enumerate(peers)
    ]
    for c in second:
        c.start()
    got2[f] = sent2[f]
    for c in second:
        c.wait_recv()
    for ri in range(2):
        parts = [got2[i, ri * T : ri * T + T, :].astype(F32) for i in range(NF)]
        for i, part in enumerate(butterfly(parts)):
            row = i % 4 * 2 + i // 4
            at = (ri, pl.ds(row, T, stride=R), slice(None))
            out[at] = part + series_f[at]
    for c in own + second:
        c.wait_send()

    @pl.when(has_below)
    def _():
        for c in down:
            c.wait_send()

    @pl.when(has_above)
    def _():
        for c in up:
            c.wait_send()


def per_device(series, lift_weight, lift_bias, mix_weight, mix_bias, proj_weight, proj_bias):
    n_rows = lax.axis_size("rows")
    args = (
        series,
        jnp.asarray(forward_table()),
        jnp.asarray(inverse_table()),
        jnp.asarray(place_table()),
        lift_weight,
        lift_bias[None],
        mix_weight,
        mix_bias[None],
        proj_weight.T,
        proj_bias[None],
    )
    scratch = [pltpu.VMEM(a.shape, a.dtype) for a in args]
    out = pl.pallas_call(
        functools.partial(kernel, n_rows),
        out_shape=pltpu.VMEM((2, T * R, 128), F32),
        in_specs=[pl.BlockSpec(memory_space=pltpu.HBM)] * len(args),
        out_specs=pl.BlockSpec(memory_space=pltpu.VMEM),
        scratch_shapes=scratch
        + [
            pltpu.VMEM((2, T * R, 128), F32),
            pltpu.VMEM((NF, 2 * T, 128), BF16),
            pltpu.VMEM((NF, T, 128), BF16),
            pltpu.VMEM((NF, 2 * T, 128), BF16),
            pltpu.VMEM((2, NF, T, 128), BF16),
            pltpu.VMEM((12 * C, 256), BF16),
            pltpu.VMEM((NG, 12 * C, 128), BF16),
            pltpu.VMEM((32, 128), F32),
            pltpu.VMEM((8, O), F32),
            pltpu.VMEM((128, G * O), BF16),
            pltpu.VMEM((1024, 256), BF16),
            pltpu.VMEM((N // 2 + 2, 10 * C, 128), BF16),
            pltpu.VMEM((NF, 2 * T, 128), BF16),
            pltpu.VMEM((NF, 2 * T, 128), BF16),
            pltpu.SemaphoreType.DMA((len(args),)),
            pltpu.SemaphoreType.DMA((NF - 1,)),
            pltpu.SemaphoreType.DMA((NF - 1,)),
            pltpu.SemaphoreType.DMA((2, NF)),
            pltpu.SemaphoreType.DMA((2, NF)),
            pltpu.SemaphoreType.DMA((NF - 1,)),
            pltpu.SemaphoreType.DMA((NF - 1,)),
        ],
        compiler_params=pltpu.CompilerParams(
            collective_id=0, has_side_effects=True, vmem_limit_bytes=56 * 1024 * 1024
        ),
    )(*args)
    return jnp.concatenate((out[0], out[1]), axis=1).reshape(T, 1, R, 256)


def solution(mesh):
    return jax.shard_map(
        per_device,
        mesh=mesh,
        in_specs=(P("frames", None, "rows", None), P(), P(), P(), P(), P(), P()),
        out_specs=P("frames", None, "rows", None),
        check_vma=False,
    )
```
